256 devices in a mesh: group: 16 (over z, x_hi), fsdp: 16 (over y, x_lo, core).
Axes of the slice: x: 4 (x_hi: 2, x_lo: 2; x = x_hi * 2 + x_lo), y: 4, z: 8, core: 2. Of those that a mesh axis runs over, the one named last changes fastest.
Arguments:
- mol_qkv: bfloat16 [128, 128, 3, 4096], P('group', None, None, 'fsdp'), may hold values from -12 to 12
- pair_list: int32 [256, 3], replicated, may hold values from 0 to 15, as said below
- head_proj: bfloat16 [32, 128, 256], P('fsdp'), may hold values from -0.5 to 0.5
- head_out: float32 [32, 256], P('fsdp'), may hold values from -0.375 to 0.375
- labels: int32 [256], P('group'), may hold values 0 or 1
Outputs:
- mol_grad: bfloat16 [128, 128, 3, 4096], P('group', None, None, 'fsdp')
- pair_logits: float32 [256], P('group')
- mean_loss: float32 [], replicated
The draws below stay inside these ranges and needn't reach their ends.
Inputs may be any that keep to these rules, and one draw needn't show every extreme that they name: `pair_list`: pair p belongs to owner p // 16; column 0 is the first molecule's index among the owner's 8 molecules, column 1 the group index that holds the second molecule, column 2 its index among that holder's 8 molecules; molecule m is held by group m // 8. `pair_list`: among one owner's pairs, at most 2 take their second molecule from any one holder, and those name at most 1 different molecules; every owner reaches both bounds.
All inputs are finite; a program needn't handle non-finite values. No bound on the sum of `labels` on one device may be relied on, other than what follows from the above.
Results may differ from the reference program's by a relative error of at most 0.0075.
Values may be sent and summed in bfloat16 or wider, within the bound.
No kernel may reach another device: no remote copies, remote signals or barrier semaphores. Data moves between devices by JAX's collectives and lax.ppermute only.
A program may use at most 128 MiB of HBM per device.

```python
import jax
import jax.numpy as jnp
from jax import lax

HEADS = 32
HD = 128
R = 256
L = 128
MOL_DEV = 8
MOLS = 128
PAIR_DEV = 16
PAIRS = 256
CAP_PAIR = 2
CAP_MOL = 1


def draw_mol_qkv(key, part):
    keys = jax.random.split(jax.random.fold_in(key, 11), 1)
    shape = (MOLS, L, 3, HEADS * HD)
    values = jax.random.normal(keys[0], shape, jnp.float32)
    return jnp.clip(values, -6.0, 6.0).astype(jnp.bfloat16)


def draw_pair_list(key, part):
    keys = jax.random.split(jax.random.fold_in(key, 23), 7)
    owners = PAIRS // PAIR_DEV
    position = jnp.arange(PAIR_DEV, dtype=jnp.int32)[None, :]
    hub_holder = jax.random.randint(keys[0], (owners, 1), 0, owners)
    offset_base = jax.random.randint(keys[1], (owners, 1), 0, owners - 1)
    other_holder = (hub_holder + 1 + (position - CAP_PAIR + offset_base) % (owners - 1)) % owners
    holder = jnp.where(position < CAP_PAIR, hub_holder, other_holder)
    base_mol = jax.random.randint(keys[2], (owners, 1), 0, MOL_DEV)
    hub_member = (base_mol + position % CAP_MOL) % MOL_DEV
    random_member = jax.random.randint(keys[3], (owners, PAIR_DEV), 0, MOL_DEV)
    member = jnp.where(position < CAP_PAIR, hub_member, random_member)
    first_mol = jnp.minimum(jax.random.randint(keys[4], (owners, PAIR_DEV), 0, MOL_DEV), jax.random.randint(keys[5], (owners, PAIR_DEV), 0, MOL_DEV))
    shuffle_keys = jax.random.randint(keys[6], (owners, PAIR_DEV), 0, 4 * PAIR_DEV) * PAIR_DEV + position
    shuffle = jnp.argsort(shuffle_keys, axis=1, stable=True)
    table = jnp.stack([first_mol, holder, member], axis=2)
    table = jnp.take_along_axis(table, shuffle[:, :, None], axis=1)
    return table.reshape(PAIRS, 3).astype(jnp.int32)


def touch_ends(result, rng, low, high):
    longest = result.shape.index(max(result.shape))
    spots = []
    for shift in (0, 1):
        where = [jax.random.randint(jax.random.fold_in(rng, axis), (), 0, length) for axis, length in enumerate(result.shape)]
        where[longest] = (where[longest] + shift) % result.shape[longest]
        spots.append(tuple(where))
    return result.at[spots[0]].set(low).at[spots[1]].set(high)


def shard_levels(rng, dims, cuts, smallest, largest):
    def one(axis_at, parts):
        draws = jax.random.uniform(jax.random.fold_in(jax.random.fold_in(rng, 6), axis_at), (parts,), jnp.float32, smallest / len(cuts), largest / len(cuts))
        return jnp.repeat(jnp.exp(draws), dims[axis_at] // parts).reshape((-1,) + (1,) * (len(dims) - axis_at - 1))

    loudness = one(*cuts[0])
    for cut in cuts[1:]:
        loudness = loudness * one(*cut)
    return loudness


def scatter_about(key, extent, scale, reach, shards=(), kind=jnp.bfloat16):
    result = jax.random.normal(key, extent, jnp.float32) * scale
    if len(shards) > 0:
        result = shard_levels(key, extent, shards, -0.22, 0.18) * result
    return jnp.clip(result, min=-reach, max=reach).astype(kind)


def setup_inputs(seed: int = 0) -> dict:
    arg_keys = jax.random.split(jax.random.key(seed), 6)
    return {
        "mol_qkv": draw_mol_qkv(jax.random.fold_in(arg_keys[5], 71), 0),
        "pair_list": draw_pair_list(jax.random.fold_in(arg_keys[5], 71), 0),
        "head_proj": scatter_about(arg_keys[2], (HEADS, HD, R), HD ** -0.5, 0.5, ((0, 16),)),
        "head_out": scatter_about(arg_keys[3], (HEADS, R), R ** -0.5, 0.375, ((0, 16),), jnp.float32),
        "labels": touch_ends((jax.random.randint(arg_keys[4], (PAIRS,), 0, 2) < 1).astype(jnp.int32), jax.random.fold_in(arg_keys[4], 1), 0, 1),
    }


loss_scale = 8192.0


def split_heads(rows_in, component, heads, head_dim):
    return rows_in[:, :, component].reshape(rows_in.shape[0], rows_in.shape[1], heads, head_dim)


def forward(query_rows, key_rows, value_rows, head_proj, head_out, inv_root, length):
    scores = jnp.einsum("plhd,pmhd->phlm", query_rows.astype(jnp.float32), key_rows.astype(jnp.float32)) * inv_root
    row_max = jnp.max(scores, axis=-1, keepdims=True)
    lifted = jnp.exp(scores - row_max)
    attn_weights = lifted / jnp.sum(lifted, axis=-1, keepdims=True)
    weights_bf = attn_weights.astype(jnp.bfloat16)
    context = jnp.einsum("phlm,pmhd->plhd", weights_bf.astype(jnp.float32), value_rows.astype(jnp.float32)).astype(jnp.bfloat16)
    hidden = jnp.einsum("plhd,hdr->plhr", context.astype(jnp.float32), head_proj.astype(jnp.float32))
    partial_value = jnp.sum(jax.nn.silu(hidden) * head_out[None, None], axis=(1, 2, 3)) / length
    return partial_value, (attn_weights, weights_bf, hidden)


def backward(query_rows, key_rows, value_rows, head_proj, head_out, saved, grad_out, inv_root, length):
    attn_weights, weights_bf, hidden = saved
    sigmoid_h = jax.nn.sigmoid(hidden)
    silu_slope = sigmoid_h * (1.0 + hidden * (1.0 - sigmoid_h))
    dhidden = (grad_out[:, None, None, None] / length * head_out[None, None] * silu_slope).astype(jnp.bfloat16)
    dcontext = jnp.einsum("plhr,hdr->plhd", dhidden.astype(jnp.float32), head_proj.astype(jnp.float32)).astype(jnp.bfloat16)
    dvalues = jnp.einsum("phlm,plhd->pmhd", weights_bf.astype(jnp.float32), dcontext.astype(jnp.float32))
    dweights = jnp.einsum("plhd,pmhd->phlm", dcontext.astype(jnp.float32), value_rows.astype(jnp.float32))
    dscores = (attn_weights * (dweights - jnp.sum(dweights * attn_weights, axis=-1, keepdims=True)) * inv_root).astype(jnp.bfloat16)
    dqueries = jnp.einsum("phlm,pmhd->plhd", dscores.astype(jnp.float32), key_rows.astype(jnp.float32))
    dkey_rows = jnp.einsum("phlm,plhd->pmhd", dscores.astype(jnp.float32), query_rows.astype(jnp.float32))
    return dqueries, dkey_rows, dvalues


def reference(mol_qkv, pair_list, head_proj, head_out, labels):
    inv_root = HD ** -0.5
    owners = PAIRS // PAIR_DEV
    blocks = pair_list.reshape(owners, PAIR_DEV, 3)
    block_labels_all = labels.reshape(owners, PAIR_DEV)
    position = jnp.arange(PAIR_DEV, dtype=jnp.int32)

    def per_block(accum, inputs):
        block_rows, block_labels, owner = inputs
        first_mol = (owner * MOL_DEV + block_rows[:, 0]).astype(jnp.int32)
        second_mol = (block_rows[:, 1] * MOL_DEV + block_rows[:, 2]).astype(jnp.int32)
        own_rows = mol_qkv[first_mol]
        partner_rows = mol_qkv[second_mol]
        qa, ka, va = [split_heads(own_rows, c, HEADS, HD) for c in range(3)]
        qb, kb, vb = [split_heads(partner_rows, c, HEADS, HD) for c in range(3)]
        part_ab, saved_ab = forward(qa, kb, vb, head_proj, head_out, inv_root, L)
        part_ba, saved_ba = forward(qb, ka, va, head_proj, head_out, inv_root, L)
        logits = part_ab + part_ba
        targets = block_labels.astype(jnp.float32)
        loss_terms = jax.nn.softplus(logits) - targets * logits
        grad_out = (jax.nn.sigmoid(logits) - targets) * loss_scale
        dq_a, dk_b, dv_b = backward(qa, kb, vb, head_proj, head_out, saved_ab, grad_out, inv_root, L)
        dq_b, dk_a, dv_a = backward(qb, ka, va, head_proj, head_out, saved_ba, grad_out, inv_root, L)
        grad_first = jnp.stack([dq_a, dk_a, dv_a], axis=2).reshape(PAIR_DEV, L, 3, HEADS * HD)
        grad_second = jnp.stack([dq_b, dk_b, dv_b], axis=2).reshape(PAIR_DEV, L, 3, HEADS * HD)
        matches = second_mol[:, None] == second_mol[None, :]
        earlier = matches & (position[None, :] < position[:, None])
        leading = jnp.logical_not(jnp.any(earlier, axis=1))
        key_sums = jnp.einsum("pq,qlcz->plcz", matches.astype(jnp.float32), grad_second, precision=lax.Precision.HIGHEST)
        rounded = lax.optimization_barrier(key_sums.astype(jnp.bfloat16)).astype(jnp.float32)
        partner_term = jnp.where(leading[:, None, None, None], rounded, jnp.zeros_like(rounded))
        accum = accum.at[first_mol].add(grad_first)
        accum = accum.at[second_mol].add(partner_term)
        return accum, (logits, jnp.sum(loss_terms))

    accum0 = jnp.zeros((MOLS, L, 3, HEADS * HD), jnp.float32)
    accum, (logits_all, loss_sums) = lax.scan(per_block, accum0, (blocks, block_labels_all, jnp.arange(owners, dtype=jnp.int32)))
    return accum.astype(jnp.bfloat16), logits_all.reshape(PAIRS), jnp.sum(loss_sums) / PAIRS
```

```python
import functools

import jax
import jax.numpy as jnp
from jax import lax
from jax.experimental import pallas as pl
from jax.experimental.pallas import tpu as pltpu
from jax.sharding import PartitionSpec as P

loss_scale = 8192.0
VMEM_BYTES = 48 * 1024 * 1024
F32 = jnp.float32
BF16 = jnp.bfloat16
SMEM_SPEC = pl.BlockSpec(memory_space=pltpu.SMEM)
VMEM_SPEC = pl.BlockSpec(memory_space=pltpu.VMEM)
ANY_SPEC = pl.BlockSpec(memory_space=pl.ANY)


def params():
    return pltpu.CompilerParams(vmem_limit_bytes=VMEM_BYTES)


def mm(a, b, ca, cb):
    return lax.dot_general(a, b, (((ca,), (cb,)), ((), ())), preferred_element_type=F32)


def pick_kernel(head, hd, member_ref, mol_ref, out_ref, sems):
    slots = out_ref.shape[0]
    copies = []
    for s in range(slots):
        copies.append(
            pltpu.make_async_copy(
                mol_ref.at[member_ref[s], :, :, pl.ds(head * hd, hd)], out_ref.at[s], sems.at[s]
            )
        )
    for c in copies:
        c.start()
    for c in copies:
        c.wait()


def pick(member, mol, head, hd):
    slots = member.shape[0]
    _, parts, length, _ = mol.shape
    return pl.pallas_call(
        functools.partial(pick_kernel, head, hd),
        out_shape=jax.ShapeDtypeStruct((slots, parts, length, hd), mol.dtype),
        in_specs=[SMEM_SPEC, ANY_SPEC],
        out_specs=ANY_SPEC,
        scratch_shapes=[pltpu.SemaphoreType.DMA((slots,))],
        compiler_params=params(),
        name="pick_rows",
    )(member, mol)


def pair_kernel(group, inv_root, first_ref, slot_ref, mol_ref, inc_ref, proj_ref, out_w_ref, prev_ref, gf_ref, gs_ref, lp_ref):
    pairs = gf_ref.shape[0]
    length = gf_ref.shape[2]
    proj = proj_ref[0]
    readout = out_w_ref[...] * (1.0 / length)

    def step(i, carry):
        units = []
        ids = []
        for j in range(group):
            p = i * group + j
            a = first_ref[p]
            s = slot_ref[p]
            ids.append(p)
            units.append((mol_ref[a, 0], inc_ref[s, 1], inc_ref[s, 2]))
            units.append((inc_ref[s, 0], mol_ref[a, 1], mol_ref[a, 2]))
        scores = [mm(q, k, 1, 1) for q, k, _ in units]
        weights = []
        for sc in scores:
            top = jnp.max(sc, axis=1, keepdims=True)
            lifted = jnp.exp((sc - top) * inv_root)
            weights.append(lifted * (1.0 / jnp.sum(lifted, axis=1, keepdims=True)))
        weights_bf = [w.astype(BF16) for w in weights]
        context = jnp.concatenate(
            [mm(w, u[2], 1, 0).astype(BF16) for w, u in zip(weights_bf, units)], axis=0
        )
        hidden = mm(context, proj, 1, 0)
        sig = 0.5 + 0.5 * jnp.tanh(0.5 * hidden)
        act = hidden * sig
        slope = sig + act * (1.0 - sig)
        dhidden = (slope * readout).astype(BF16)
        for j, p in enumerate(ids):
            rows = jnp.sum(act[2 * j * length : (2 * j + 2) * length], axis=0, keepdims=True)
            total = jnp.sum(rows * readout, axis=1, keepdims=True)
            lp_ref[pl.ds(p, 1), :] = prev_ref[pl.ds(p, 1), :] + jnp.broadcast_to(total, (1, lp_ref.shape[1]))
        dcontext_all = mm(dhidden, proj, 1, 1).astype(BF16)
        dcontext = [dcontext_all[n * length : (n + 1) * length] for n in range(len(units))]
        dvalues = [mm(w, d, 0, 0) for w, d in zip(weights_bf, dcontext)]
        dweights = [mm(d, u[2], 1, 1) for d, u in zip(dcontext, units)]
        dscores = []
        for w, dw in zip(weights, dweights):
            inner = jnp.sum(dw * w, axis=1, keepdims=True)
            dscores.append((w * (dw - inner) * inv_root).astype(BF16))
        dqueries = [mm(d, u[1], 1, 0) for d, u in zip(dscores, units)]
        dkeys = [mm(d, u[0], 0, 0) for d, u in zip(dscores, units)]
        for j, p in enumerate(ids):
            ab, ba = 2 * j, 2 * j + 1
            gf_ref[p, 0] = dqueries[ab].astype(BF16)
            gf_ref[p, 1] = dkeys[ba].astype(BF16)
            gf_ref[p, 2] = dvalues[ba].astype(BF16)
            gs_ref[p, 0] = dqueries[ba].astype(BF16)
            gs_ref[p, 1] = dkeys[ab].astype(BF16)
            gs_ref[p, 2] = dvalues[ab].astype(BF16)
        return carry

    lax.fori_loop(0, pairs // group, step, 0)


def pair_grads(first, slot, mol, inc, proj, readout, prev, head, hd):
    pairs = first.shape[0]
    mols, parts, length, _ = mol.shape
    grad_shape = jax.ShapeDtypeStruct((pairs, parts, length, hd), BF16)
    width = proj.shape[2]
    return pl.pallas_call(
        functools.partial(pair_kernel, 2, hd ** (-0.5)),
        grid=(1,),
        out_shape=(grad_shape, grad_shape, jax.ShapeDtypeStruct((pairs, 128), F32)),
        in_specs=[
            SMEM_SPEC,
            SMEM_SPEC,
            pl.BlockSpec((mols, parts, length, hd), lambda i: (0, 0, 0, head)),
            VMEM_SPEC,
            pl.BlockSpec((1, hd, width), lambda i: (head, 0, 0)),
            VMEM_SPEC,
            VMEM_SPEC,
        ],
        out_specs=(VMEM_SPEC, VMEM_SPEC, VMEM_SPEC),
        compiler_params=params(),
        name="pair_grads",
    )(first, slot, mol, inc, proj, readout, prev)


def grad_scale(logits, target):
    return (0.5 + 0.5 * jnp.tanh(0.5 * logits) - target) * loss_scale


def second_kernel(slot_ref, lead_ref, mate_ref, logits_ref, target_ref, gs_ref, out_ref, scale_ref):
    pairs, parts = gs_ref.shape[:2]
    scale_ref[...] = grad_scale(logits_ref[...], target_ref[...])

    def step(p, carry):
        slot = slot_ref[p]
        mate = mate_ref[p]
        own = scale_ref[pl.ds(p, 1), :]

        @pl.when((lead_ref[p] == 1) & (mate < 0))
        def single():
            for c in range(parts):
                out_ref[slot, c] = (own * gs_ref[p, c].astype(F32)).astype(BF16)

        @pl.when((lead_ref[p] == 1) & (mate >= 0))
        def double():
            other_at = jnp.maximum(mate, 0)
            other = scale_ref[pl.ds(other_at, 1), :]
            for c in range(parts):
                out_ref[slot, c] = (
                    own * gs_ref[p, c].astype(F32) + other * gs_ref[other_at, c].astype(F32)
                ).astype(BF16)

        return carry

    lax.fori_loop(0, pairs, step, 0)


def second_terms(slot, lead, mate, logits, target, gs, slots):
    pairs, parts, length, hd = gs.shape
    return pl.pallas_call(
        second_kernel,
        out_shape=jax.ShapeDtypeStruct((slots, parts, length, hd), BF16),
        in_specs=[SMEM_SPEC] * 3 + [VMEM_SPEC] * 3,
        out_specs=VMEM_SPEC,
        scratch_shapes=[pltpu.VMEM(logits.shape, F32)],
        compiler_params=params(),
        name="second_terms",
    )(slot, lead, mate, logits, target, gs)


def first_kernel(first_ref, logits_ref, target_ref, gf_ref, own_ref, scale_ref):
    pairs, parts = gf_ref.shape[:2]
    scale_ref[...] = grad_scale(logits_ref[...], target_ref[...])
    own_ref[...] = jnp.zeros_like(own_ref)

    def step(p, carry):
        a = first_ref[p]
        own = scale_ref[pl.ds(p, 1), :]
        for c in range(parts):
            own_ref[a, c] += own * gf_ref[p, c].astype(F32)
        return carry

    lax.fori_loop(0, pairs, step, 0)


def first_terms(first, logits, target, gf, mols):
    pairs, parts, length, hd = gf.shape
    return pl.pallas_call(
        first_kernel,
        out_shape=jax.ShapeDtypeStruct((mols, parts, length, hd), F32),
        in_specs=[SMEM_SPEC] + [VMEM_SPEC] * 3,
        out_specs=VMEM_SPEC,
        scratch_shapes=[pltpu.VMEM(logits.shape, F32)],
        compiler_params=params(),
        name="first_terms",
    )(first, logits, target, gf)


def add_returned(code_ref, back_ref, sum_ref):
    slots, parts = back_ref.shape[:2]

    def step(s, carry):
        m = code_ref[s]

        @pl.when(m >= 0)
        def add():
            at = jnp.maximum(m, 0)
            for c in range(parts):
                sum_ref[at, c] += back_ref[s, c].astype(F32)

        return carry

    lax.fori_loop(0, slots, step, 0)


def finish_kernel(code_ref, back_ref, own_ref, out_ref, sum_ref):
    sum_ref[...] = own_ref[...]
    add_returned(code_ref, back_ref, sum_ref)
    out_ref[...] = sum_ref[...].astype(BF16)


def finish(code, back, own):
    mols, parts, length, hd = own.shape
    return pl.pallas_call(
        finish_kernel,
        out_shape=jax.ShapeDtypeStruct((mols, parts, length, hd), BF16),
        in_specs=[SMEM_SPEC, VMEM_SPEC, VMEM_SPEC],
        out_specs=VMEM_SPEC,
        scratch_shapes=[pltpu.VMEM(own.shape, F32)],
        compiler_params=params(),
        name="finish_head",
    )(code, back, own)


def finish_last_kernel(code_ref, back_ref, own_ref, earlier_ref, out_ref, sum_ref):
    hd = own_ref.shape[3]
    sum_ref[...] = own_ref[...]
    add_returned(code_ref, back_ref, sum_ref)
    out_ref[:, :, :, :hd] = earlier_ref[...]
    out_ref[:, :, :, hd:] = sum_ref[...].astype(BF16)


def finish_last(code, back, own, earlier):
    mols, parts, length, hd = own.shape
    return pl.pallas_call(
        finish_last_kernel,
        out_shape=jax.ShapeDtypeStruct((mols, parts, length, 2 * hd), BF16),
        in_specs=[SMEM_SPEC, VMEM_SPEC, VMEM_SPEC, VMEM_SPEC],
        out_specs=VMEM_SPEC,
        scratch_shapes=[pltpu.VMEM(own.shape, F32)],
        compiler_params=params(),
        name="finish_last_head",
    )(code, back, own, earlier)


def butterfly(value, axis, size):
    hop = 1
    while hop < size:
        value = value + lax.ppermute(value, axis, [(i, i ^ hop) for i in range(size)])
        hop *= 2
    return value


def exchange(value):
    return lax.all_to_all(value, "group", split_axis=0, concat_axis=0, tiled=True)


def local(mol_qkv, pair_list, head_proj, head_out, labels):
    groups = lax.axis_size("group")
    shards = lax.axis_size("fsdp")
    device = lax.axis_index("group")
    mols = mol_qkv.shape[0]
    hd = head_proj.shape[1]
    total_pairs = pair_list.shape[0]
    pairs = total_pairs // groups
    mol = jnp.transpose(mol_qkv, (0, 2, 1, 3))

    blocks = pair_list.T.reshape(3, groups, pairs)
    code = jnp.max(jnp.where(blocks[1] == device, blocks[2], -1), axis=1)
    member = jnp.maximum(code, 0)
    mine = lax.dynamic_index_in_dim(blocks, device, 1, keepdims=False)
    first, slot = mine[0], mine[1]
    place = jnp.arange(pairs, dtype=jnp.int32)
    same = slot[:, None] == slot[None, :]
    lead = jnp.logical_not(jnp.any(same & (place[None, :] < place[:, None]), axis=1)).astype(jnp.int32)
    mate = jnp.max(jnp.where(same & (place[None, :] > place[:, None]), place[None, :], -1), axis=1)

    inc0 = exchange(pick(member, mol, 0, hd))
    inc1 = exchange(pick(member, mol, 1, hd))
    none = jnp.zeros((pairs, 128), F32)
    gf0, gs0, part0 = pair_grads(first, slot, mol, inc0, head_proj, head_out[0:1], none, 0, hd)
    gf1, gs1, part1 = pair_grads(first, slot, mol, inc1, head_proj, head_out[1:2], part0, 1, hd)
    logits_wide = butterfly(part1, "fsdp", shards)
    targets = labels.astype(F32)
    target_wide = jnp.broadcast_to(targets[:, None], logits_wide.shape)

    out0 = second_terms(slot, lead, mate, logits_wide, target_wide, gs0, groups)
    out1 = second_terms(slot, lead, mate, logits_wide, target_wide, gs1, groups)
    back0 = exchange(out0)
    back1 = exchange(out1)
    own0 = first_terms(first, logits_wide, target_wide, gf0, mols)
    own1 = first_terms(first, logits_wide, target_wide, gf1, mols)

    logits = logits_wide[:, 0]
    loss_terms = jax.nn.softplus(logits) - targets * logits
    mean_loss = butterfly(jnp.sum(loss_terms), "group", groups) / total_pairs

    half = finish(code, back0, own0)
    grads = finish_last(code, back1, own1, half)
    mol_grad = jnp.transpose(grads, (0, 2, 1, 3))
    return (mol_grad, logits, mean_loss)


def solution(mesh):
    placed = (
        P("group", None, None, "fsdp"),
        P(),
        P("fsdp", None, None),
        P("fsdp", None),
        P("group"),
    )
    return jax.shard_map(
        local,
        mesh=mesh,
        in_specs=placed,
        out_specs=(P("group", None, None, "fsdp"), P("group"), P()),
        check_vma=False,
    )
```

```python
import functools

import jax
import jax.numpy as jnp
from jax import lax
from jax.experimental import pallas as pl
from jax.experimental.pallas import tpu as pltpu
from jax.sharding import PartitionSpec as P

loss_scale = 8192.0
VMEM_BYTES = 24 * 1024 * 1024
SECOND_BYTES = 54 * 1024 * 1024
VMEM_ALL = 60 * 1024 * 1024
F32 = jnp.float32
BF16 = jnp.bfloat16
SMEM_SPEC = pl.BlockSpec(memory_space=pltpu.SMEM)
VMEM_SPEC = pl.BlockSpec(memory_space=pltpu.VMEM)
ANY_SPEC = pl.BlockSpec(memory_space=pl.ANY)


def params(limit=VMEM_BYTES):
    return pltpu.CompilerParams(vmem_limit_bytes=limit)


def mm(a, b, ca, cb):
    return lax.dot_general(a, b, (((ca,), (cb,)), ((), ())), preferred_element_type=F32)

HBM_SPEC = pl.BlockSpec(memory_space=pltpu.HBM)


def pick_kernel(start, parts, member_ref, mol_ref, out_ref, sems):
    slots = out_ref.shape[0]
    copies = []
    for s in range(slots):
        copies.append(
            pltpu.make_async_copy(
                mol_ref.at[member_ref[s], pl.ds(start, parts)], out_ref.at[s], sems.at[s]
            )
        )
    for c in copies:
        c.start()
    for c in copies:
        c.wait()


def pick(member, mol, start, parts):
    slots = member.shape[0]
    _, _, length, width = mol.shape
    return pl.pallas_call(
        functools.partial(pick_kernel, start, parts),
        out_shape=jax.ShapeDtypeStruct((slots, parts, length, width), mol.dtype),
        in_specs=[SMEM_SPEC, HBM_SPEC],
        out_specs=HBM_SPEC,
        scratch_shapes=[pltpu.SemaphoreType.DMA((slots,))],
        compiler_params=params(VMEM_ALL),
        name="pick_rows",
    )(member, mol)


def lanes(ref_value, head, hd):
    return ref_value[:, head * hd : (head + 1) * hd]


def weights_of(query, key, inv_root):
    scores = mm(query, key, 1, 1)
    top = jnp.max(scores, axis=1, keepdims=True)
    lifted = jnp.exp((scores - top) * inv_root)
    return lifted * (1.0 / jnp.sum(lifted, axis=1, keepdims=True))


def hidden_of(weights_bf, units, proj):
    context = jnp.concatenate([mm(w, u[2], 1, 0).astype(BF16) for w, u in zip(weights_bf, units)], axis=0)
    hidden = mm(context, proj, 1, 0)
    sig = 0.5 + 0.5 * jnp.tanh(0.5 * hidden)
    return sig, hidden * sig


def add_logits(ids, acts, readouts, length, prev_ref, lp_ref):
    for j, p in enumerate(ids):
        rows = [
            jnp.sum(act[j * length : (j + 1) * length], axis=0, keepdims=True) * readout
            for act, readout in zip(acts, readouts)
        ]
        total = jnp.sum(sum(rows[1:], rows[0]), axis=1, keepdims=True)
        total = jnp.broadcast_to(total, (1, lp_ref.shape[1]))
        if prev_ref is not None:
            total = total + prev_ref[pl.ds(p, 1), :]
        lp_ref[pl.ds(p, 1), :] = total


def forward_units(units, proj_ref, inv_root):
    heads = proj_ref.shape[0]
    weights = [[weights_of(u[0], u[1], inv_root) for u in units[h]] for h in range(heads)]
    weights_bf = [[w.astype(BF16) for w in weights[h]] for h in range(heads)]
    sigs, acts = zip(*[hidden_of(weights_bf[h], units[h], proj_ref[h]) for h in range(heads)])
    return weights, weights_bf, sigs, acts


def direction_units(ids, refs, heads, hd):
    return [[tuple(r(p)[:, h * hd : (h + 1) * hd] for r in refs) for p in ids] for h in range(heads)]


def backward_units(units, weights, weights_bf, sigs, acts, proj_ref, readouts, inv_root, store):
    heads = len(units)
    length = units[0][0][0].shape[0]
    count = len(units[0])
    dcontext = []
    for h in range(heads):
        slope = sigs[h] + acts[h] * (1.0 - sigs[h])
        dhidden = (slope * readouts[h]).astype(BF16)
        whole = mm(dhidden, proj_ref[h], 1, 1).astype(BF16)
        dcontext.append([whole[j * length : (j + 1) * length] for j in range(count)])
    for h in range(heads):
        for j in range(count):
            store(j, h, 2, mm(weights_bf[h][j], dcontext[h][j], 0, 0))
    dweights = [[mm(dcontext[h][j], units[h][j][2], 1, 1) for j in range(count)] for h in range(heads)]
    dscores = []
    for h in range(heads):
        row = []
        for j in range(count):
            w, dw = weights[h][j], dweights[h][j]
            inner = jnp.sum(dw * w, axis=1, keepdims=True)
            row.append((w * (dw - inner) * inv_root).astype(BF16))
        dscores.append(row)
    for h in range(heads):
        for j in range(count):
            store(j, h, 0, mm(dscores[h][j], units[h][j][1], 1, 0))
            store(j, h, 1, mm(dscores[h][j], units[h][j][0], 0, 0))


def outward_kernel(group, first_ref, slot_ref, mol_ref, kv_ref, proj_ref, readout_ref, dq_ref, dkv_ref, lp_ref):
    pairs, length, _ = dq_ref.shape
    heads, hd, _ = proj_ref.shape
    inv_root = hd ** (-0.5)
    readouts = [readout_ref[h : h + 1, :] * (1.0 / length) for h in range(heads)]

    def step(i, carry):
        ids = [i * group + j for j in range(group)]
        units = direction_units(
            ids,
            (lambda p: mol_ref[first_ref[p], 0], lambda p: kv_ref[slot_ref[p], 0], lambda p: kv_ref[slot_ref[p], 1]),
            heads,
            hd,
        )
        weights, weights_bf, sigs, acts = forward_units(units, proj_ref, inv_root)
        add_logits(ids, acts, readouts, length, None, lp_ref)

        def store(j, h, part, value):
            value = value.astype(BF16)
            if part == 0:
                dq_ref[ids[j], :, h * hd : (h + 1) * hd] = value
            else:
                dkv_ref[ids[j], part - 1, :, h * hd : (h + 1) * hd] = value

        backward_units(units, weights, weights_bf, sigs, acts, proj_ref, readouts, inv_root, store)
        return carry

    lax.fori_loop(0, pairs // group, step, 0)


def inward_logits_kernel(group, first_ref, slot_ref, mol_ref, q_ref, proj_ref, readout_ref, prev_ref, lp_ref):
    pairs = lp_ref.shape[0]
    length = mol_ref.shape[2]
    heads, hd, _ = proj_ref.shape
    inv_root = hd ** (-0.5)
    readouts = [readout_ref[h : h + 1, :] * (1.0 / length) for h in range(heads)]

    def step(i, carry):
        ids = [i * group + j for j in range(group)]
        units = direction_units(
            ids,
            (lambda p: q_ref[slot_ref[p], 0], lambda p: mol_ref[first_ref[p], 1], lambda p: mol_ref[first_ref[p], 2]),
            heads,
            hd,
        )
        acts = forward_units(units, proj_ref, inv_root)[3]
        add_logits(ids, acts, readouts, length, prev_ref, lp_ref)
        return carry

    lax.fori_loop(0, pairs // group, step, 0)


def inward_kernel(group, first_ref, slot_ref, mol_ref, q_ref, proj_ref, readout_ref, dq_ref, dkv_ref):
    pairs, length, _ = dq_ref.shape
    heads, hd, _ = proj_ref.shape
    inv_root = hd ** (-0.5)
    readouts = [readout_ref[h : h + 1, :] * (1.0 / length) for h in range(heads)]

    def step(i, carry):
        ids = [i * group + j for j in range(group)]
        units = direction_units(
            ids,
            (lambda p: q_ref[slot_ref[p], 0], lambda p: mol_ref[first_ref[p], 1], lambda p: mol_ref[first_ref[p], 2]),
            heads,
            hd,
        )
        weights, weights_bf, sigs, acts = forward_units(units, proj_ref, inv_root)

        def store(j, h, part, value):
            value = value.astype(BF16)
            if part == 0:
                dq_ref[ids[j], :, h * hd : (h + 1) * hd] = value
            else:
                dkv_ref[ids[j], part - 1, :, h * hd : (h + 1) * hd] = value

        backward_units(units, weights, weights_bf, sigs, acts, proj_ref, readouts, inv_root, store)
        return carry

    lax.fori_loop(0, pairs // group, step, 0)


def wide(pairs):
    return jax.ShapeDtypeStruct((pairs, 128), F32)


def grads_shape(pairs, mol):
    _, parts, length, width = mol.shape
    return (
        jax.ShapeDtypeStruct((pairs, length, width), BF16),
        jax.ShapeDtypeStruct((pairs, parts - 1, length, width), BF16),
    )


def pair_cost(share, terms):
    return pl.CostEstimate(flops=int(2.7e9 * share), bytes_accessed=terms, transcendentals=0)


def outward(first, slot, mol, kv, proj, readout):
    pairs = first.shape[0]
    return pl.pallas_call(
        functools.partial(outward_kernel, 2),
        out_shape=grads_shape(pairs, mol) + (wide(pairs),),
        in_specs=[SMEM_SPEC] * 2 + [VMEM_SPEC] * 4,
        out_specs=(VMEM_SPEC,) * 3,
        compiler_params=params(),
        name="outward_grads",
    )(first, slot, mol, kv, proj, readout)


def inward_logits(first, slot, mol, q, proj, readout, prev):
    return pl.pallas_call(
        functools.partial(inward_logits_kernel, 2),
        out_shape=jax.ShapeDtypeStruct(prev.shape, F32),
        in_specs=[SMEM_SPEC] * 2 + [VMEM_SPEC] * 5,
        out_specs=VMEM_SPEC,
        compiler_params=params(),
        name="inward_logits",
    )(first, slot, mol, q, proj, readout, prev)


def inward(first, slot, mol, q, proj, readout):
    pairs = first.shape[0]
    return pl.pallas_call(
        functools.partial(inward_kernel, 2),
        out_shape=grads_shape(pairs, mol),
        in_specs=[SMEM_SPEC] * 2 + [VMEM_SPEC] * 4,
        out_specs=(VMEM_SPEC,) * 2,
        compiler_params=params(),
        name="inward_grads",
    )(first, slot, mol, q, proj, readout)


def grad_scale(logits, target):
    scale = (0.5 + 0.5 * jnp.tanh(0.5 * logits) - target) * loss_scale
    return jnp.concatenate([scale, scale], axis=1)


def second_kernel(slot_ref, lead_ref, mate_ref, logits_ref, target_ref, gs_ref, out_ref, scale_ref, hold_ref, sems):
    pairs, parts = gs_ref.shape[:2]
    scale_ref[...] = grad_scale(logits_ref[...], target_ref[...])

    def send(p):
        return pltpu.make_async_copy(hold_ref.at[p], out_ref.at[slot_ref[p]], sems.at[p])

    def step(p, carry):
        mate = mate_ref[p]
        own = scale_ref[pl.ds(p, 1), :]

        @pl.when((lead_ref[p] == 1) & (mate < 0))
        def single():
            for c in range(parts):
                hold_ref[p, c] = (own * gs_ref[p, c].astype(F32)).astype(BF16)
            send(p).start()

        @pl.when((lead_ref[p] == 1) & (mate >= 0))
        def double():
            other_at = jnp.maximum(mate, 0)
            other = scale_ref[pl.ds(other_at, 1), :]
            for c in range(parts):
                hold_ref[p, c] = (
                    own * gs_ref[p, c].astype(F32) + other * gs_ref[other_at, c].astype(F32)
                ).astype(BF16)
            send(p).start()

        return carry

    lax.fori_loop(0, pairs, step, 0)

    def land(p, carry):
        @pl.when(lead_ref[p] == 1)
        def wait():
            send(p).wait()

        return carry

    lax.fori_loop(0, pairs, land, 0)


def second_terms(slot, lead, mate, logits, target, gs, slots):
    pairs, parts, length, width = gs.shape
    return pl.pallas_call(
        second_kernel,
        out_shape=jax.ShapeDtypeStruct((slots, parts, length, width), BF16),
        in_specs=[SMEM_SPEC] * 3 + [VMEM_SPEC] * 3,
        out_specs=HBM_SPEC,
        scratch_shapes=[
            pltpu.VMEM((pairs, width), F32),
            pltpu.VMEM((pairs, parts, length, width), BF16),
            pltpu.SemaphoreType.DMA((pairs,)),
        ],
        compiler_params=params(SECOND_BYTES),
        name="second_terms",
    )(slot, lead, mate, logits, target, gs)


def finish_kernel(first_ref, code_ref, logits_ref, target_ref, own_ref, back_ref, *rest):
    out_ref, sum_ref, scale_ref = rest[-3:]
    pairs = own_ref.shape[0]
    slots = back_ref.shape[0]
    scale_ref[...] = grad_scale(logits_ref[...], target_ref[...])
    sum_ref[...] = jnp.zeros_like(sum_ref)

    def own_step(p, carry):
        sum_ref[first_ref[p]] += scale_ref[pl.ds(p, 1), :] * own_ref[p, 0].astype(F32)
        return carry

    def back_step(s, carry):
        m = code_ref[s]

        @pl.when(m >= 0)
        def add():
            sum_ref[jnp.maximum(m, 0)] += back_ref[s, 0].astype(F32)

        return carry

    lax.fori_loop(0, pairs, own_step, 0)
    lax.fori_loop(0, slots, back_step, 0)
    out_ref[:, 0] = sum_ref[...].astype(BF16)


def finish(first, code, logits, target, own, back, mols, start, whole):
    pairs, parts, length, width = own.shape
    slots = back.shape[0]
    part = lambda i: (0, i, 0, 0)
    operands = (first, code, logits, target, own, back)
    in_specs = [SMEM_SPEC] * 2 + [VMEM_SPEC] * 2
    in_specs += [pl.BlockSpec((pairs, 1, length, width), part), pl.BlockSpec((slots, 1, length, width), part)]
    aliases = {}
    if whole is not None:
        operands += (whole,)
        in_specs += [HBM_SPEC]
        aliases = {len(operands) - 1: 0}
    return pl.pallas_call(
        finish_kernel,
        grid=(parts,),
        out_shape=jax.ShapeDtypeStruct((mols, 3, length, width), BF16),
        in_specs=in_specs,
        out_specs=pl.BlockSpec((mols, 1, length, width), lambda i: (0, start + i, 0, 0)),
        scratch_shapes=[pltpu.VMEM((mols, length, width), F32), pltpu.VMEM((pairs, width), F32)],
        input_output_aliases=aliases,
        compiler_params=params(),
        name="finish_parts",
    )(*operands)


def hop(value, axis, size, change):
    return lax.ppermute(value, axis, [(i, change(i)) for i in range(size)])


def butterfly(value, axis, size):
    step = 1
    while step < size:
        value = value + hop(value, axis, size, lambda i: i ^ step)
        step *= 2
    return value


def sum_shards(value, size):
    quarter = size // 4
    step = 1
    while step < quarter:
        value = value + hop(value, "fsdp", size, lambda i: i ^ step)
        step *= 2
    near, far, last = [
        hop(value, "fsdp", size, lambda i: (i + k * quarter) % size) for k in (1, 2, 3)
    ]
    return (value + far) + (near + last)


def exchange(value):
    return lax.all_to_all(value, "group", split_axis=0, concat_axis=0, tiled=True)


def local(mol_qkv, pair_list, head_proj, head_out, labels):
    groups = lax.axis_size("group")
    shards = lax.axis_size("fsdp")
    device = lax.axis_index("group")
    mols = mol_qkv.shape[0]
    total_pairs = pair_list.shape[0]
    pairs = total_pairs // groups
    mol = jnp.transpose(mol_qkv, (0, 2, 1, 3))

    blocks = pair_list.T.reshape(3, groups, pairs)
    code = jnp.max(jnp.where(blocks[1] == device, blocks[2], -1), axis=1)
    member = jnp.maximum(code, 0)
    mine = lax.dynamic_index_in_dim(blocks, device, 1, keepdims=False)
    first, slot = mine[0], mine[1]
    place = jnp.arange(pairs, dtype=jnp.int32)
    same = slot[:, None] == slot[None, :]
    lead = jnp.logical_not(jnp.any(same & (place[None, :] < place[:, None]), axis=1)).astype(jnp.int32)
    mate = jnp.max(jnp.where(same & (place[None, :] > place[:, None]), place[None, :], -1), axis=1)

    kv = exchange(pick(member, mol, 1, 2))
    q = exchange(pick(member, mol, 0, 1))
    out_dq, out_dkv, part = outward(first, slot, mol, kv, head_proj, head_out)
    part = inward_logits(first, slot, mol, q, head_proj, head_out, part)
    logits_wide = sum_shards(part, shards)
    targets = labels.astype(F32)
    target_wide = jnp.broadcast_to(targets[:, None], logits_wide.shape)

    back_kv = exchange(second_terms(slot, lead, mate, logits_wide, target_wide, out_dkv, groups))
    in_dq, in_dkv = inward(first, slot, mol, q, head_proj, head_out)
    logits = logits_wide[:, 0]
    loss_terms = jax.nn.softplus(logits) - targets * logits
    mean_loss = butterfly(jnp.sum(loss_terms), "group", groups) / total_pairs
    in_dq, mean_loss = lax.optimization_barrier((in_dq, mean_loss))
    back_q = exchange(second_terms(slot, lead, mate, logits_wide, target_wide, in_dq[:, None], groups))

    grads = finish(first, code, logits_wide, target_wide, in_dkv, back_kv, mols, 1, None)
    grads = finish(first, code, logits_wide, target_wide, out_dq[:, None], back_q, mols, 0, grads)
    mol_grad = jnp.transpose(grads, (0, 2, 1, 3))
    return (mol_grad, logits, mean_loss)


def solution(mesh):
    placed = (
        P("group", None, None, "fsdp"),
        P(),
        P("fsdp", None, None),
        P("fsdp", None),
        P("group"),
    )
    return jax.shard_map(
        local,
        mesh=mesh,
        in_specs=placed,
        out_specs=(P("group", None, None, "fsdp"), P("group"), P()),
        check_vma=False,
    )
```

```python
import functools

import jax
import jax.numpy as jnp
from jax import lax
from jax.experimental import pallas as pl
from jax.experimental.pallas import tpu as pltpu
from jax.sharding import PartitionSpec as P

loss_scale = 8192.0
VMEM_BYTES = 24 * 1024 * 1024
SECOND_BYTES = 54 * 1024 * 1024
VMEM_ALL = 60 * 1024 * 1024
F32 = jnp.float32
BF16 = jnp.bfloat16
SMEM_SPEC = pl.BlockSpec(memory_space=pltpu.SMEM)
VMEM_SPEC = pl.BlockSpec(memory_space=pltpu.VMEM)
ANY_SPEC = pl.BlockSpec(memory_space=pl.ANY)


def params(limit=VMEM_BYTES):
    return pltpu.CompilerParams(vmem_limit_bytes=limit)


def mm(a, b, ca, cb):
    return lax.dot_general(a, b, (((ca,), (cb,)), ((), ())), preferred_element_type=F32)

HBM_SPEC = pl.BlockSpec(memory_space=pltpu.HBM)


def pick_kernel(member_ref, mol_ref, out_ref, hold_ref, in_sems, out_sems):
    slots = out_ref.shape[0]
    mols = mol_ref.shape[0]
    loads = [pltpu.make_async_copy(mol_ref.at[m], hold_ref.at[m], in_sems.at[m]) for m in range(mols)]
    for c in loads:
        c.start()
    for c in loads:
        c.wait()
    copies = [
        pltpu.make_async_copy(hold_ref.at[member_ref[s]], out_ref.at[s], out_sems.at[s]) for s in range(slots)
    ]
    for c in copies:
        c.start()
    for c in copies:
        c.wait()


def pick(member, mol):
    slots = member.shape[0]
    return pl.pallas_call(
        pick_kernel,
        out_shape=jax.ShapeDtypeStruct((slots,) + mol.shape[1:], mol.dtype),
        in_specs=[SMEM_SPEC, HBM_SPEC],
        out_specs=HBM_SPEC,
        scratch_shapes=[
            pltpu.VMEM(mol.shape, mol.dtype),
            pltpu.SemaphoreType.DMA((mol.shape[0],)),
            pltpu.SemaphoreType.DMA((slots,)),
        ],
        compiler_params=params(VMEM_ALL),
        name="pick_rows",
    )(member, mol)


def load_units(ids, first_ref, slot_ref, mol_ref, inc_ref, heads, hd, directions):
    units = []
    for h in range(heads):
        cols = slice(h * hd, (h + 1) * hd)
        for j, p in enumerate(ids):
            a, s = first_ref[p], slot_ref[p]
            for d in directions:
                if d == 0:
                    rows = (mol_ref[a, 0, :, cols], inc_ref[s, 1, :, cols], inc_ref[s, 2, :, cols])
                else:
                    rows = (inc_ref[s, 0, :, cols], mol_ref[a, 1, :, cols], mol_ref[a, 2, :, cols])
                units.append((j, d, h) + rows)
    return units


def forward_kernel(group, first_ref, slot_ref, mol_ref, inc_ref, proj_ref, readout_ref, lp_ref, w_ref, dh_ref):
    pairs = lp_ref.shape[0]
    length = mol_ref.shape[2]
    heads, hd, _ = proj_ref.shape
    inv_root = hd ** (-0.5)
    readouts = [readout_ref[h : h + 1, :] * (1.0 / length) for h in range(heads)]

    def step(i, carry):
        ids = [i * group + j for j in range(group)]
        units = load_units(ids, first_ref, slot_ref, mol_ref, inc_ref, heads, hd, (0, 1))
        scores = [mm(u[4], u[3], 1, 1) for u in units]
        weights = []
        for sc in scores:
            lifted = jnp.exp((sc - jnp.max(sc, axis=0, keepdims=True)) * inv_root)
            weights.append(lifted * (1.0 / jnp.sum(lifted, axis=0, keepdims=True)))
        context = [mm(w.astype(BF16), u[5], 0, 0).astype(BF16) for w, u in zip(weights, units)]
        count = len(units) // heads
        totals = [None] * group
        dhidden = []
        for h in range(heads):
            hidden = mm(jnp.concatenate(context[h * count : (h + 1) * count], axis=0), proj_ref[h], 1, 0)
            sig = 0.5 + 0.5 * jnp.tanh(0.5 * hidden)
            act = hidden * sig
            for j in range(group):
                rows = jnp.sum(act[2 * j * length : (2 * j + 2) * length], axis=0, keepdims=True) * readouts[h]
                totals[j] = rows if totals[j] is None else totals[j] + rows
            dhidden.append(((sig + act * (1.0 - sig)) * readouts[h]).astype(BF16))
        for j, p in enumerate(ids):
            total = jnp.sum(totals[j], axis=1, keepdims=True)
            lp_ref[pl.ds(p, 1), :] = jnp.broadcast_to(total, (1, lp_ref.shape[1]))
        for n, (j, d, h, *_) in enumerate(units):
            at = n - h * count
            w_ref[d, ids[j], h] = weights[n]
            dh_ref[d, ids[j], h] = dhidden[h][at * length : (at + 1) * length]
        return carry

    lax.fori_loop(0, pairs // group, step, 0)


def forward(first, slot, mol, inc, proj, readout):
    pairs = first.shape[0]
    length = mol.shape[2]
    heads, _, width = proj.shape
    return pl.pallas_call(
        functools.partial(forward_kernel, min(8, pairs)),
        out_shape=(
            jax.ShapeDtypeStruct((pairs, 128), F32),
            jax.ShapeDtypeStruct((2, pairs, heads, length, length), F32),
            jax.ShapeDtypeStruct((2, pairs, heads, length, width), BF16),
        ),
        in_specs=[SMEM_SPEC] * 2 + [VMEM_SPEC] * 4,
        out_specs=(VMEM_SPEC,) * 3,
        compiler_params=params(),
        name="pair_forward",
    )(first, slot, mol, inc, proj, readout)


def backward_kernel(direction, group, first_ref, slot_ref, mol_ref, inc_ref, proj_ref, w_ref, dh_ref, dq_ref, dkv_ref):
    pairs, length, _ = dq_ref.shape
    heads, hd, _ = proj_ref.shape
    inv_root = hd ** (-0.5)

    def step(i, carry):
        ids = [i * group + j for j in range(group)]
        units = load_units(ids, first_ref, slot_ref, mol_ref, inc_ref, heads, hd, (direction,))
        weights = [w_ref[0, ids[u[0]], u[2]] for u in units]
        dcontext = []
        for h in range(heads):
            dhidden = jnp.concatenate([dh_ref[0, p, h] for p in ids], axis=0)
            whole = mm(dhidden, proj_ref[h], 1, 1).astype(BF16)
            dcontext += [whole[j * length : (j + 1) * length] for j in range(group)]
        dvalues = [mm(w.astype(BF16), dc, 1, 0).astype(BF16) for w, dc in zip(weights, dcontext)]
        dweights = [mm(u[5], dc, 1, 1) for u, dc in zip(units, dcontext)]
        dscores = []
        for w, dw in zip(weights, dweights):
            inner = jnp.sum(dw * w, axis=0, keepdims=True)
            dscores.append((w * (dw - inner) * inv_root).astype(BF16))
        dqueries = [mm(ds, u[4], 0, 0).astype(BF16) for ds, u in zip(dscores, units)]
        dkeys = [mm(ds, u[3], 1, 0).astype(BF16) for ds, u in zip(dscores, units)]
        for n, (j, _, h, *_) in enumerate(units):
            cols = slice(h * hd, (h + 1) * hd)
            dq_ref[ids[j], :, cols] = dqueries[n]
            dkv_ref[ids[j], 0, :, cols] = dkeys[n]
            dkv_ref[ids[j], 1, :, cols] = dvalues[n]
        return carry

    lax.fori_loop(0, pairs // group, step, 0)


def backward(direction, first, slot, mol, inc, proj, weights, dhidden):
    pairs = first.shape[0]
    _, parts, length, width = mol.shape
    here = lambda i: (direction, 0, 0, 0, 0)
    return pl.pallas_call(
        functools.partial(backward_kernel, direction, min(16, pairs)),
        grid=(1,),
        out_shape=(
            jax.ShapeDtypeStruct((pairs, length, width), BF16),
            jax.ShapeDtypeStruct((pairs, parts - 1, length, width), BF16),
        ),
        in_specs=[SMEM_SPEC] * 2
        + [VMEM_SPEC] * 3
        + [pl.BlockSpec((1,) + weights.shape[1:], here), pl.BlockSpec((1,) + dhidden.shape[1:], here)],
        out_specs=(VMEM_SPEC,) * 2,
        compiler_params=params(),
        name="pair_backward",
    )(first, slot, mol, inc, proj, weights, dhidden)


def grad_scale(logits, target):
    scale = (0.5 + 0.5 * jnp.tanh(0.5 * logits) - target) * loss_scale
    return jnp.concatenate([scale, scale], axis=1)


def second_kernel(slot_ref, lead_ref, mate_ref, logits_ref, target_ref, dq_ref, dkv_ref, out_ref, scale_ref, hold_ref, sems):
    pairs = dq_ref.shape[0]
    scale_ref[...] = grad_scale(logits_ref[...], target_ref[...])

    def send(p):
        return pltpu.make_async_copy(hold_ref.at[p], out_ref.at[slot_ref[p]], sems.at[p])

    def part(p, c):
        return (dq_ref[p] if c == 0 else dkv_ref[p, c - 1]).astype(F32)

    def step(p, carry):
        mate = mate_ref[p]
        own = scale_ref[pl.ds(p, 1), :]

        @pl.when((lead_ref[p] == 1) & (mate < 0))
        def single():
            for c in range(3):
                hold_ref[p, c] = (own * part(p, c)).astype(BF16)
            send(p).start()

        @pl.when((lead_ref[p] == 1) & (mate >= 0))
        def double():
            at = jnp.maximum(mate, 0)
            other = scale_ref[pl.ds(at, 1), :]
            for c in range(3):
                hold_ref[p, c] = (own * part(p, c) + other * part(at, c)).astype(BF16)
            send(p).start()

        return carry

    lax.fori_loop(0, pairs, step, 0)

    def land(p, carry):
        @pl.when(lead_ref[p] == 1)
        def wait():
            send(p).wait()

        return carry

    lax.fori_loop(0, pairs, land, 0)


def second_terms(slot, lead, mate, logits, target, dq, dkv, slots):
    pairs, length, width = dq.shape
    return pl.pallas_call(
        second_kernel,
        out_shape=jax.ShapeDtypeStruct((slots, 3, length, width), BF16),
        in_specs=[SMEM_SPEC] * 3 + [VMEM_SPEC] * 4,
        out_specs=HBM_SPEC,
        scratch_shapes=[
            pltpu.VMEM((pairs, width), F32),
            pltpu.VMEM((pairs, 3, length, width), BF16),
            pltpu.SemaphoreType.DMA((pairs,)),
        ],
        compiler_params=params(SECOND_BYTES),
        name="second_terms",
    )(slot, lead, mate, logits, target, dq, dkv)


def first_kernel(first_ref, logits_ref, target_ref, dq_ref, dkv_ref, own_ref, scale_ref):
    pairs = dq_ref.shape[0]
    scale_ref[...] = grad_scale(logits_ref[...], target_ref[...])
    own_ref[...] = jnp.zeros_like(own_ref)

    def step(p, carry):
        a = first_ref[p]
        scale = scale_ref[pl.ds(p, 1), :]
        for c in range(3):
            own_ref[a, c] += scale * (dq_ref[p] if c == 0 else dkv_ref[p, c - 1]).astype(F32)
        return carry

    lax.fori_loop(0, pairs, step, 0)


def first_terms(first, logits, target, dq, dkv, mols):
    pairs, length, width = dq.shape
    return pl.pallas_call(
        first_kernel,
        out_shape=jax.ShapeDtypeStruct((mols, 3, length, width), F32),
        in_specs=[SMEM_SPEC] + [VMEM_SPEC] * 4,
        out_specs=VMEM_SPEC,
        scratch_shapes=[pltpu.VMEM((pairs, width), F32)],
        compiler_params=params(),
        name="first_terms",
    )(first, logits, target, dq, dkv)


def finish_kernel(code_ref, own_ref, back_ref, out_ref, sum_ref):
    slots = back_ref.shape[0]
    sum_ref[...] = own_ref[:, 0]

    def step(s, carry):
        m = code_ref[s]

        @pl.when(m >= 0)
        def add():
            sum_ref[jnp.maximum(m, 0)] += back_ref[s, 0].astype(F32)

        return carry

    lax.fori_loop(0, slots, step, 0)
    out_ref[:, 0] = sum_ref[...].astype(BF16)


def finish(code, own, back):
    mols, parts, length, width = own.shape
    slots = back.shape[0]
    part = lambda i: (0, i, 0, 0)
    return pl.pallas_call(
        finish_kernel,
        grid=(parts,),
        out_shape=jax.ShapeDtypeStruct(own.shape, BF16),
        in_specs=[
            SMEM_SPEC,
            pl.BlockSpec((mols, 1, length, width), part),
            pl.BlockSpec((slots, 1, length, width), part),
        ],
        out_specs=pl.BlockSpec((mols, 1, length, width), part),
        scratch_shapes=[pltpu.VMEM((mols, length, width), F32)],
        compiler_params=params(),
        name="finish_parts",
    )(code, own, back)


def hop(value, axis, size, change):
    return lax.ppermute(value, axis, [(i, change(i)) for i in range(size)])


def sum_quarter(value, recv):
    near, far, last = recv
    return (value + far) + (near + last)


def quarters(value, size):
    quarter = size // 4
    return [hop(value, "fsdp", size, lambda i: (i + k * quarter) % size) for k in (1, 2, 3)]


def sum_shards(value, size):
    step = 1
    while step < size // 4:
        value = value + hop(value, "fsdp", size, lambda i: i ^ step)
        step *= 2
    return sum_quarter(value, quarters(value, size))


def sum_shards_beside(value, size, first_work, second_work):
    step = 1
    while step < size // 8:
        value = value + hop(value, "fsdp", size, lambda i: i ^ step)
        step *= 2
    recv = hop(value, "fsdp", size, lambda i: i ^ step)
    done = first_work(value)
    recv, done = lax.optimization_barrier((recv, done))
    value = value + recv
    recv = quarters(value, size)
    more = second_work(value)
    recv, more = lax.optimization_barrier((recv, more))
    return sum_quarter(value, recv), done, more


def sum_groups(value, groups, shards):
    where = [(g * shards + f, (g ^ f) * shards + f) for g in range(groups) for f in range(shards)]
    return sum_shards(lax.ppermute(value, ("group", "fsdp"), where), shards)


def exchange(value):
    return lax.all_to_all(value, "group", split_axis=0, concat_axis=0, tiled=True)


def local(mol_qkv, pair_list, head_proj, head_out, labels):
    groups = lax.axis_size("group")
    shards = lax.axis_size("fsdp")
    device = lax.axis_index("group")
    mols = mol_qkv.shape[0]
    total_pairs = pair_list.shape[0]
    pairs = total_pairs // groups
    mol = jnp.transpose(mol_qkv, (0, 2, 1, 3))

    blocks = pair_list.T.reshape(3, groups, pairs)
    code = jnp.max(jnp.where(blocks[1] == device, blocks[2], -1), axis=1)
    mine = lax.dynamic_index_in_dim(blocks, device, 1, keepdims=False)
    first, slot = mine[0], mine[1]
    place = jnp.arange(pairs, dtype=jnp.int32)
    same = slot[:, None] == slot[None, :]
    lead = jnp.logical_not(jnp.any(same & (place[None, :] < place[:, None]), axis=1)).astype(jnp.int32)
    mate = jnp.max(jnp.where(same & (place[None, :] > place[:, None]), place[None, :], -1), axis=1)
    targets = labels.astype(F32)
    target_wide = jnp.broadcast_to(targets[:, None], (pairs, 128))

    inc = exchange(pick(jnp.maximum(code, 0), mol))
    inc, lead, mate, target_wide = lax.optimization_barrier((inc, lead, mate, target_wide))
    part, weights, dhidden = forward(first, slot, mol, inc, head_proj, head_out)

    def grads(direction):
        def work(after):
            index, _ = lax.optimization_barrier((first, after))
            return backward(direction, index, slot, mol, inc, head_proj, weights, dhidden)

        return work

    logits_wide, (dq_a, dkv_b), (dq_b, dkv_a) = sum_shards_beside(part, shards, grads(0), grads(1))

    back = exchange(second_terms(slot, lead, mate, logits_wide, target_wide, dq_b, dkv_b, groups))
    own = first_terms(first, logits_wide, target_wide, dq_a, dkv_a, mols)
    logits = logits_wide[:, 0]
    loss_terms = jax.nn.softplus(logits) - targets * logits
    mean_loss = sum_groups(jnp.sum(loss_terms), groups, shards) / total_pairs
    mol_grad = jnp.transpose(finish(code, own, back), (0, 2, 1, 3))
    return (mol_grad, logits, mean_loss)


def solution(mesh):
    placed = (
        P("group", None, None, "fsdp"),
        P(),
        P("fsdp", None, None),
        P("fsdp", None),
        P("group"),
    )
    return jax.shard_map(
        local,
        mesh=mesh,
        in_specs=placed,
        out_specs=(P("group", None, None, "fsdp"), P("group"), P()),
        check_vma=False,
    )
```

```python
import functools

import jax
import jax.numpy as jnp
from jax import lax
from jax.experimental import pallas as pl
from jax.experimental.pallas import tpu as pltpu
from jax.sharding import PartitionSpec as P

loss_scale = 8192.0
VMEM_BYTES = 24 * 1024 * 1024
SECOND_BYTES = 40 * 1024 * 1024
VMEM_ALL = 60 * 1024 * 1024
F32 = jnp.float32
BF16 = jnp.bfloat16
SMEM_SPEC = pl.BlockSpec(memory_space=pltpu.SMEM)
VMEM_SPEC = pl.BlockSpec(memory_space=pltpu.VMEM)
ANY_SPEC = pl.BlockSpec(memory_space=pl.ANY)


def params(limit=VMEM_BYTES):
    return pltpu.CompilerParams(vmem_limit_bytes=limit)


def mm(a, b, ca, cb):
    return lax.dot_general(a, b, (((ca,), (cb,)), ((), ())), preferred_element_type=F32)

HBM_SPEC = pl.BlockSpec(memory_space=pltpu.HBM)


def pick_kernel(member_ref, mol_ref, out_ref, hold_ref, in_sems, out_sems):
    slots = out_ref.shape[0]
    mols = mol_ref.shape[0]
    loads = [pltpu.make_async_copy(mol_ref.at[m], hold_ref.at[m], in_sems.at[m]) for m in range(mols)]
    for c in loads:
        c.start()
    for c in loads:
        c.wait()
    copies = [
        pltpu.make_async_copy(hold_ref.at[member_ref[s]], out_ref.at[s], out_sems.at[s]) for s in range(slots)
    ]
    for c in copies:
        c.start()
    for c in copies:
        c.wait()


def pick(member, mol):
    slots = member.shape[0]
    return pl.pallas_call(
        pick_kernel,
        out_shape=jax.ShapeDtypeStruct((slots,) + mol.shape[1:], mol.dtype),
        in_specs=[SMEM_SPEC, HBM_SPEC],
        out_specs=HBM_SPEC,
        scratch_shapes=[
            pltpu.VMEM(mol.shape, mol.dtype),
            pltpu.SemaphoreType.DMA((mol.shape[0],)),
            pltpu.SemaphoreType.DMA((slots,)),
        ],
        compiler_params=params(VMEM_ALL),
        name="pick_rows",
    )(member, mol)


def load_units(ids, first_ref, slot_ref, mol_ref, inc_ref, heads, hd, directions):
    units = []
    for h in range(heads):
        cols = slice(h * hd, (h + 1) * hd)
        for j, p in enumerate(ids):
            a, s = first_ref[p], slot_ref[p]
            for d in directions:
                if d == 0:
                    rows = (mol_ref[a, 0, :, cols], inc_ref[s, 1, :, cols], inc_ref[s, 2, :, cols])
                else:
                    rows = (inc_ref[s, 0, :, cols], mol_ref[a, 1, :, cols], mol_ref[a, 2, :, cols])
                units.append((j, d, h) + rows)
    return units


def forward_kernel(group, first_ref, slot_ref, mol_ref, inc_ref, proj_ref, readout_ref, lp_ref, w_ref, dh_ref):
    pairs = lp_ref.shape[0]
    length = mol_ref.shape[2]
    heads, hd, _ = proj_ref.shape
    inv_root = hd ** (-0.5)
    readouts = [readout_ref[h : h + 1, :] * (1.0 / length) for h in range(heads)]

    def step(i, carry):
        ids = [i * group + j for j in range(group)]
        units = load_units(ids, first_ref, slot_ref, mol_ref, inc_ref, heads, hd, (0, 1))
        scores = [mm(u[4], u[3], 1, 1) for u in units]
        weights = []
        for sc in scores:
            lifted = jnp.exp((sc - jnp.max(sc, axis=0, keepdims=True)) * inv_root)
            weights.append(lifted * (1.0 / jnp.sum(lifted, axis=0, keepdims=True)))
        context = [mm(w.astype(BF16), u[5], 0, 0).astype(BF16) for w, u in zip(weights, units)]
        count = len(units) // heads
        totals = [None] * group
        dhidden = []
        for h in range(heads):
            hidden = mm(jnp.concatenate(context[h * count : (h + 1) * count], axis=0), proj_ref[h], 1, 0)
            sig = 0.5 + 0.5 * jnp.tanh(0.5 * hidden)
            act = hidden * sig
            for j in range(group):
                rows = jnp.sum(act[2 * j * length : (2 * j + 2) * length], axis=0, keepdims=True) * readouts[h]
                totals[j] = rows if totals[j] is None else totals[j] + rows
            dhidden.append(((sig + act * (1.0 - sig)) * readouts[h]).astype(BF16))
        for j, p in enumerate(ids):
            total = jnp.sum(totals[j], axis=1, keepdims=True)
            lp_ref[pl.ds(p, 1), :] = jnp.broadcast_to(total, (1, lp_ref.shape[1]))
        for n, (j, d, h, *_) in enumerate(units):
            at = n - h * count
            w_ref[d, ids[j], h] = weights[n]
            dh_ref[d, ids[j], h] = dhidden[h][at * length : (at + 1) * length]
        return carry

    lax.fori_loop(0, pairs // group, step, 0)


def forward(first, slot, mol, inc, proj, readout):
    pairs = first.shape[0]
    length = mol.shape[2]
    heads, _, width = proj.shape
    return pl.pallas_call(
        functools.partial(forward_kernel, min(8, pairs)),
        out_shape=(
            jax.ShapeDtypeStruct((pairs, 128), F32),
            jax.ShapeDtypeStruct((2, pairs, heads, length, length), F32),
            jax.ShapeDtypeStruct((2, pairs, heads, length, width), BF16),
        ),
        in_specs=[SMEM_SPEC] * 2 + [VMEM_SPEC] * 4,
        out_specs=(VMEM_SPEC,) * 3,
        compiler_params=params(),
        name="pair_forward",
    )(first, slot, mol, inc, proj, readout)


def backward_kernel(direction, group, first_ref, slot_ref, mol_ref, inc_ref, proj_ref, w_ref, dh_ref, dq_ref, dkv_ref):
    pairs, length, _ = dq_ref.shape
    heads, hd, _ = proj_ref.shape
    inv_root = hd ** (-0.5)

    def step(i, carry):
        ids = [i * group + j for j in range(group)]
        units = load_units(ids, first_ref, slot_ref, mol_ref, inc_ref, heads, hd, (direction,))
        weights = [w_ref[0, ids[u[0]], u[2]] for u in units]
        dcontext = []
        for h in range(heads):
            dhidden = jnp.concatenate([dh_ref[0, p, h] for p in ids], axis=0)
            whole = mm(dhidden, proj_ref[h], 1, 1).astype(BF16)
            dcontext += [whole[j * length : (j + 1) * length] for j in range(group)]
        dvalues = [mm(w.astype(BF16), dc, 1, 0).astype(BF16) for w, dc in zip(weights, dcontext)]
        dweights = [mm(u[5], dc, 1, 1) for u, dc in zip(units, dcontext)]
        dscores = []
        for w, dw in zip(weights, dweights):
            inner = jnp.sum(dw * w, axis=0, keepdims=True)
            dscores.append((w * (dw - inner) * inv_root).astype(BF16))
        dqueries = [mm(ds, u[4], 0, 0).astype(BF16) for ds, u in zip(dscores, units)]
        dkeys = [mm(ds, u[3], 1, 0).astype(BF16) for ds, u in zip(dscores, units)]
        for n, (j, _, h, *_) in enumerate(units):
            cols = slice(h * hd, (h + 1) * hd)
            dq_ref[ids[j], :, cols] = dqueries[n]
            dkv_ref[ids[j], 0, :, cols] = dkeys[n]
            dkv_ref[ids[j], 1, :, cols] = dvalues[n]
        return carry

    lax.fori_loop(0, pairs // group, step, 0)


def backward(direction, first, slot, mol, inc, proj, weights, dhidden):
    pairs = first.shape[0]
    _, parts, length, width = mol.shape
    here = lambda i: (direction, 0, 0, 0, 0)
    return pl.pallas_call(
        functools.partial(backward_kernel, direction, min(16, pairs)),
        grid=(1,),
        out_shape=(
            jax.ShapeDtypeStruct((pairs, length, width), BF16),
            jax.ShapeDtypeStruct((pairs, parts - 1, length, width), BF16),
        ),
        in_specs=[SMEM_SPEC] * 2
        + [VMEM_SPEC] * 3
        + [pl.BlockSpec((1,) + weights.shape[1:], here), pl.BlockSpec((1,) + dhidden.shape[1:], here)],
        out_specs=(VMEM_SPEC,) * 2,
        compiler_params=params(),
        name="pair_backward",
    )(first, slot, mol, inc, proj, weights, dhidden)


def grad_scale(logits, target):
    scale = (0.5 + 0.5 * jnp.tanh(0.5 * logits) - target) * loss_scale
    return jnp.concatenate([scale, scale], axis=1)


def second_kernel(slot_ref, lead_ref, mate_ref, logits_ref, target_ref, dq_ref, dkv_ref, out_ref, scale_ref, hold_ref, sems):
    pairs = dq_ref.shape[0]
    scale_ref[...] = grad_scale(logits_ref[...], target_ref[...])

    def send(p):
        return pltpu.make_async_copy(hold_ref.at[p], out_ref.at[slot_ref[p]], sems.at[p])

    def part(p, c):
        return (dq_ref[p] if c == 0 else dkv_ref[p, c - 1]).astype(F32)

    def step(p, carry):
        mate = mate_ref[p]
        own = scale_ref[pl.ds(p, 1), :]

        @pl.when((lead_ref[p] == 1) & (mate < 0))
        def single():
            for c in range(3):
                hold_ref[p, c] = (own * part(p, c)).astype(BF16)
            send(p).start()

        @pl.when((lead_ref[p] == 1) & (mate >= 0))
        def double():
            at = jnp.maximum(mate, 0)
            other = scale_ref[pl.ds(at, 1), :]
            for c in range(3):
                hold_ref[p, c] = (own * part(p, c) + other * part(at, c)).astype(BF16)
            send(p).start()

        return carry

    lax.fori_loop(0, pairs, step, 0)

    def land(p, carry):
        @pl.when(lead_ref[p] == 1)
        def wait():
            send(p).wait()

        return carry

    lax.fori_loop(0, pairs, land, 0)


def second_terms(slot, lead, mate, logits, target, dq, dkv, slots):
    pairs, length, width = dq.shape
    return pl.pallas_call(
        second_kernel,
        out_shape=jax.ShapeDtypeStruct((slots, 3, length, width), BF16),
        in_specs=[SMEM_SPEC] * 3 + [VMEM_SPEC] * 4,
        out_specs=HBM_SPEC,
        scratch_shapes=[
            pltpu.VMEM((pairs, width), F32),
            pltpu.VMEM((pairs, 3, length, width), BF16),
            pltpu.SemaphoreType.DMA((pairs,)),
        ],
        compiler_params=params(SECOND_BYTES),
        name="second_terms",
    )(slot, lead, mate, logits, target, dq, dkv)


def first_kernel(first_ref, logits_ref, target_ref, dq_ref, dkv_ref, own_ref, scale_ref):
    pairs = dq_ref.shape[0]
    scale_ref[...] = grad_scale(logits_ref[...], target_ref[...])
    own_ref[...] = jnp.zeros_like(own_ref)

    def step(p, carry):
        a = first_ref[p]
        scale = scale_ref[pl.ds(p, 1), :]
        for c in range(3):
            own_ref[a, c] += scale * (dq_ref[p] if c == 0 else dkv_ref[p, c - 1]).astype(F32)
        return carry

    lax.fori_loop(0, pairs, step, 0)


def first_terms(first, logits, target, dq, dkv, mols):
    pairs, length, width = dq.shape
    return pl.pallas_call(
        first_kernel,
        out_shape=jax.ShapeDtypeStruct((mols, 3, length, width), F32),
        in_specs=[SMEM_SPEC] + [VMEM_SPEC] * 4,
        out_specs=VMEM_SPEC,
        scratch_shapes=[pltpu.VMEM((pairs, width), F32)],
        compiler_params=params(),
        name="first_terms",
    )(first, logits, target, dq, dkv)


def finish_kernel(code_ref, own_ref, back_ref, out_ref, sum_ref):
    slots = back_ref.shape[0]
    sum_ref[...] = own_ref[:, 0]

    def step(s, carry):
        m = code_ref[s]

        @pl.when(m >= 0)
        def add():
            sum_ref[jnp.maximum(m, 0)] += back_ref[s, 0].astype(F32)

        return carry

    lax.fori_loop(0, slots, step, 0)
    out_ref[:, 0] = sum_ref[...].astype(BF16)


def finish(code, own, back):
    mols, parts, length, width = own.shape
    slots = back.shape[0]
    part = lambda i: (0, i, 0, 0)
    return pl.pallas_call(
        finish_kernel,
        grid=(parts,),
        out_shape=jax.ShapeDtypeStruct(own.shape, BF16),
        in_specs=[
            SMEM_SPEC,
            pl.BlockSpec((mols, 1, length, width), part),
            pl.BlockSpec((slots, 1, length, width), part),
        ],
        out_specs=pl.BlockSpec((mols, 1, length, width), part),
        scratch_shapes=[pltpu.VMEM((mols, length, width), F32)],
        compiler_params=params(VMEM_ALL),
        name="finish_parts",
    )(code, own, back)


def hop(value, axis, size, change):
    return lax.ppermute(value, axis, [(i, change(i)) for i in range(size)])


def sum_quarter(value, recv):
    near, far, last = recv
    return (value + far) + (near + last)


def quarters(value, size):
    quarter = size // 4
    return [hop(value, "fsdp", size, lambda i: (i + k * quarter) % size) for k in (1, 2, 3)]


def sum_shards(value, size):
    step = 1
    while step < size // 4:
        value = value + hop(value, "fsdp", size, lambda i: i ^ step)
        step *= 2
    return sum_quarter(value, quarters(value, size))


def sum_shards_beside(value, size, first_work, second_work):
    step = 1
    while step < size // 8:
        value = value + hop(value, "fsdp", size, lambda i: i ^ step)
        step *= 2
    recv = hop(value, "fsdp", size, lambda i: i ^ step)
    done = first_work(value)
    recv, done = lax.optimization_barrier((recv, done))
    value = value + recv
    recv = quarters(value, size)
    more = second_work(value)
    recv, more = lax.optimization_barrier((recv, more))
    return sum_quarter(value, recv), done, more


def turn_groups(value, groups, shards):
    where = [(g * shards + f, (g ^ f) * shards + f) for g in range(groups) for f in range(shards)]
    return lax.ppermute(value, ("group", "fsdp"), where)


def exchange(value):
    return lax.all_to_all(value, "group", split_axis=0, concat_axis=0, tiled=True)


def local(mol_qkv, pair_list, head_proj, head_out, labels):
    groups = lax.axis_size("group")
    shards = lax.axis_size("fsdp")
    device = lax.axis_index("group")
    mols = mol_qkv.shape[0]
    total_pairs = pair_list.shape[0]
    pairs = total_pairs // groups
    mol = jnp.transpose(mol_qkv, (0, 2, 1, 3))

    blocks = pair_list.T.reshape(3, groups, pairs)
    code = jnp.max(jnp.where(blocks[1] == device, blocks[2], -1), axis=1)
    mine = lax.dynamic_index_in_dim(blocks, device, 1, keepdims=False)
    first, slot = mine[0], mine[1]
    place = jnp.arange(pairs, dtype=jnp.int32)
    same = slot[:, None] == slot[None, :]
    lead = jnp.logical_not(jnp.any(same & (place[None, :] < place[:, None]), axis=1)).astype(jnp.int32)
    mate = jnp.max(jnp.where(same & (place[None, :] > place[:, None]), place[None, :], -1), axis=1)
    targets = labels.astype(F32)
    target_wide = jnp.broadcast_to(targets[:, None], (pairs, 128))

    inc = exchange(pick(jnp.maximum(code, 0), mol))
    inc, lead, mate, target_wide = lax.optimization_barrier((inc, lead, mate, target_wide))
    part, weights, dhidden = forward(first, slot, mol, inc, head_proj, head_out)

    def grads(direction):
        def work(after):
            index, _ = lax.optimization_barrier((first, after))
            return backward(direction, index, slot, mol, inc, head_proj, weights, dhidden)

        return work

    logits_wide, (dq_a, dkv_b), (dq_b, dkv_a) = sum_shards_beside(part, shards, grads(0), grads(1))

    loss_wide = jax.nn.softplus(logits_wide) - target_wide * logits_wide
    loss_moved = turn_groups(loss_wide, groups, shards)
    out = second_terms(slot, lead, mate, logits_wide, target_wide, dq_b, dkv_b, groups)
    out, loss_moved = lax.optimization_barrier((out, loss_moved))
    back = exchange(out)
    own = first_terms(first, logits_wide, target_wide, dq_a, dkv_a, mols)
    loss_sum = jnp.sum(sum_shards(loss_moved, shards)[:, 0])
    mean_loss = loss_sum / total_pairs
    logits = logits_wide[:, 0]
    mol_grad = jnp.transpose(finish(code, own, back), (0, 2, 1, 3))
    return (mol_grad, logits, mean_loss)


def solution(mesh):
    placed = (
        P("group", None, None, "fsdp"),
        P(),
        P("fsdp", None, None),
        P("fsdp", None),
        P("group"),
    )
    return jax.shard_map(
        local,
        mesh=mesh,
        in_specs=placed,
        out_specs=(P("group", None, None, "fsdp"), P("group"), P()),
        check_vma=False,
    )
```

```python
import functools

import jax
import jax.numpy as jnp
from jax import lax
from jax.experimental import pallas as pl
from jax.experimental.pallas import tpu as pltpu
from jax.sharding import PartitionSpec as P

loss_scale = 8192.0
VMEM_BYTES = 24 * 1024 * 1024
FINISH_BYTES = 48 * 1024 * 1024
SECOND_BYTES = 40 * 1024 * 1024
VMEM_ALL = 60 * 1024 * 1024
F32 = jnp.float32
BF16 = jnp.bfloat16
SMEM_SPEC = pl.BlockSpec(memory_space=pltpu.SMEM)
VMEM_SPEC = pl.BlockSpec(memory_space=pltpu.VMEM)
ANY_SPEC = pl.BlockSpec(memory_space=pl.ANY)


def params(limit=VMEM_BYTES):
    return pltpu.CompilerParams(vmem_limit_bytes=limit)


def mm(a, b, ca, cb):
    return lax.dot_general(a, b, (((ca,), (cb,)), ((), ())), preferred_element_type=F32)

HBM_SPEC = pl.BlockSpec(memory_space=pltpu.HBM)


def pick_kernel(code_ref, mol_ref, out_ref, hold_ref, in_sems, out_sems):
    slots = out_ref.shape[0]
    mols = mol_ref.shape[0]
    loads = [pltpu.make_async_copy(mol_ref.at[m], hold_ref.at[m], in_sems.at[m]) for m in range(mols)]
    for c in loads:
        c.start()
    members = [jnp.maximum(code_ref[s], 0) for s in range(slots)]
    for m in range(mols):
        loads[m].wait()
        for s in range(slots):

            @pl.when(members[s] == m)
            def send():
                pltpu.make_async_copy(hold_ref.at[m], out_ref.at[s], out_sems.at[s]).start()

    for s in range(slots):
        pltpu.make_async_copy(hold_ref.at[members[s]], out_ref.at[s], out_sems.at[s]).wait()


def pick(code, mol):
    slots = code.shape[0]
    return pl.pallas_call(
        pick_kernel,
        out_shape=jax.ShapeDtypeStruct((slots,) + mol.shape[1:], mol.dtype),
        in_specs=[SMEM_SPEC, HBM_SPEC],
        out_specs=HBM_SPEC,
        scratch_shapes=[
            pltpu.VMEM(mol.shape, mol.dtype),
            pltpu.SemaphoreType.DMA((mol.shape[0],)),
            pltpu.SemaphoreType.DMA((slots,)),
        ],
        compiler_params=params(VMEM_ALL),
        name="pick_rows",
    )(code, mol)


def load_units(ids, first_ref, slot_ref, mol_ref, inc_ref, heads, hd, directions):
    units = []
    for h in range(heads):
        cols = slice(h * hd, (h + 1) * hd)
        for j, p in enumerate(ids):
            a, s = first_ref[p], slot_ref[p]
            for d in directions:
                if d == 0:
                    rows = (mol_ref[a, 0, :, cols], inc_ref[s, 1, :, cols], inc_ref[s, 2, :, cols])
                else:
                    rows = (inc_ref[s, 0, :, cols], mol_ref[a, 1, :, cols], mol_ref[a, 2, :, cols])
                units.append((j, d, h) + rows)
    return units


def forward_kernel(group, first_ref, slot_ref, mol_ref, inc_ref, proj_ref, readout_ref, lp_ref, w_ref, dh_ref):
    pairs = lp_ref.shape[0]
    length = mol_ref.shape[2]
    heads, hd, _ = proj_ref.shape
    inv_root = hd ** (-0.5)
    readouts = [readout_ref[h : h + 1, :] * (1.0 / length) for h in range(heads)]

    def step(i, carry):
        ids = [i * group + j for j in range(group)]
        units = load_units(ids, first_ref, slot_ref, mol_ref, inc_ref, heads, hd, (0, 1))
        scores = [mm(u[4], u[3], 1, 1) for u in units]
        weights = []
        for sc in scores:
            lifted = jnp.exp((sc - jnp.max(sc, axis=0, keepdims=True)) * inv_root)
            weights.append(lifted * (1.0 / jnp.sum(lifted, axis=0, keepdims=True)))
        context = [mm(w.astype(BF16), u[5], 0, 0).astype(BF16) for w, u in zip(weights, units)]
        count = len(units) // heads
        totals = [None] * group
        dhidden = []
        for h in range(heads):
            hidden = mm(jnp.concatenate(context[h * count : (h + 1) * count], axis=0), proj_ref[h], 1, 0)
            sig = 0.5 + 0.5 * jnp.tanh(0.5 * hidden)
            act = hidden * sig
            for j in range(group):
                rows = jnp.sum(act[2 * j * length : (2 * j + 2) * length], axis=0, keepdims=True) * readouts[h]
                totals[j] = rows if totals[j] is None else totals[j] + rows
            dhidden.append(((sig + act * (1.0 - sig)) * readouts[h]).astype(BF16))
        for j, p in enumerate(ids):
            total = jnp.sum(totals[j], axis=1, keepdims=True)
            lp_ref[pl.ds(p, 1), :] = jnp.broadcast_to(total, (1, lp_ref.shape[1]))
        for n, (j, d, h, *_) in enumerate(units):
            at = n - h * count
            w_ref[d, ids[j], h] = weights[n]
            dh_ref[d, ids[j], h] = dhidden[h][at * length : (at + 1) * length]
        return carry

    lax.fori_loop(0, pairs // group, step, 0)


def forward(first, slot, mol, inc, proj, readout):
    pairs = first.shape[0]
    length = mol.shape[2]
    heads, _, width = proj.shape
    return pl.pallas_call(
        functools.partial(forward_kernel, min(8, pairs)),
        out_shape=(
            jax.ShapeDtypeStruct((pairs, 128), F32),
            jax.ShapeDtypeStruct((2, pairs, heads, length, length), F32),
            jax.ShapeDtypeStruct((2, pairs, heads, length, width), BF16),
        ),
        in_specs=[SMEM_SPEC] * 2 + [VMEM_SPEC] * 4,
        out_specs=(VMEM_SPEC,) * 3,
        compiler_params=params(),
        name="pair_forward",
    )(first, slot, mol, inc, proj, readout)


def backward_kernel(direction, group, first_ref, slot_ref, mol_ref, inc_ref, proj_ref, w_ref, dh_ref, dq_ref, dkv_ref):
    pairs, length, _ = dq_ref.shape
    heads, hd, _ = proj_ref.shape
    inv_root = hd ** (-0.5)

    def step(i, carry):
        ids = [i * group + j for j in range(group)]
        units = load_units(ids, first_ref, slot_ref, mol_ref, inc_ref, heads, hd, (direction,))
        weights = [w_ref[0, ids[u[0]], u[2]] for u in units]
        dcontext = []
        for h in range(heads):
            dhidden = jnp.concatenate([dh_ref[0, p, h] for p in ids], axis=0)
            whole = mm(dhidden, proj_ref[h], 1, 1).astype(BF16)
            dcontext += [whole[j * length : (j + 1) * length] for j in range(group)]
        dvalues = [mm(w.astype(BF16), dc, 1, 0).astype(BF16) for w, dc in zip(weights, dcontext)]
        dweights = [mm(u[5], dc, 1, 1) for u, dc in zip(units, dcontext)]
        dscores = []
        for w, dw in zip(weights, dweights):
            inner = jnp.sum(dw * w, axis=0, keepdims=True)
            dscores.append((w * (dw - inner) * inv_root).astype(BF16))
        dqueries = [mm(ds, u[4], 0, 0).astype(BF16) for ds, u in zip(dscores, units)]
        dkeys = [mm(ds, u[3], 1, 0).astype(BF16) for ds, u in zip(dscores, units)]
        for n, (j, _, h, *_) in enumerate(units):
            cols = slice(h * hd, (h + 1) * hd)
            dq_ref[ids[j], :, cols] = dqueries[n]
            dkv_ref[ids[j], 0, :, cols] = dkeys[n]
            dkv_ref[ids[j], 1, :, cols] = dvalues[n]
        return carry

    lax.fori_loop(0, pairs // group, step, 0)


def backward(direction, first, slot, mol, inc, proj, weights, dhidden):
    pairs = first.shape[0]
    _, parts, length, width = mol.shape
    here = lambda i: (direction, 0, 0, 0, 0)
    return pl.pallas_call(
        functools.partial(backward_kernel, direction, min(16, pairs)),
        grid=(1,),
        out_shape=(
            jax.ShapeDtypeStruct((pairs, length, width), BF16),
            jax.ShapeDtypeStruct((pairs, parts - 1, length, width), BF16),
        ),
        in_specs=[SMEM_SPEC] * 2
        + [VMEM_SPEC] * 3
        + [pl.BlockSpec((1,) + weights.shape[1:], here), pl.BlockSpec((1,) + dhidden.shape[1:], here)],
        out_specs=(VMEM_SPEC,) * 2,
        compiler_params=params(),
        name="pair_backward",
    )(first, slot, mol, inc, proj, weights, dhidden)


def grad_scale(logits, target):
    scale = (0.5 + 0.5 * jnp.tanh(0.5 * logits) - target) * loss_scale
    return jnp.concatenate([scale, scale], axis=1)


def second_kernel(slot_ref, lead_ref, mate_ref, logits_ref, target_ref, dq_ref, dkv_ref, out_ref, scale_ref, hold_ref, sems):
    pairs = dq_ref.shape[0]
    scale_ref[...] = grad_scale(logits_ref[...], target_ref[...])

    def send(p):
        return pltpu.make_async_copy(hold_ref.at[p], out_ref.at[slot_ref[p]], sems.at[p])

    def part(p, c):
        return (dq_ref[p] if c == 0 else dkv_ref[p, c - 1]).astype(F32)

    def step(p, carry):
        mate = mate_ref[p]
        own = scale_ref[pl.ds(p, 1), :]

        @pl.when((lead_ref[p] == 1) & (mate < 0))
        def single():
            for c in range(3):
                hold_ref[p, c] = (own * part(p, c)).astype(BF16)
            send(p).start()

        @pl.when((lead_ref[p] == 1) & (mate >= 0))
        def double():
            at = jnp.maximum(mate, 0)
            other = scale_ref[pl.ds(at, 1), :]
            for c in range(3):
                hold_ref[p, c] = (own * part(p, c) + other * part(at, c)).astype(BF16)
            send(p).start()

        return carry

    lax.fori_loop(0, pairs, step, 0)

    def land(p, carry):
        @pl.when(lead_ref[p] == 1)
        def wait():
            send(p).wait()

        return carry

    lax.fori_loop(0, pairs, land, 0)


def second_terms(slot, lead, mate, logits, target, dq, dkv, slots):
    pairs, length, width = dq.shape
    return pl.pallas_call(
        second_kernel,
        out_shape=jax.ShapeDtypeStruct((slots, 3, length, width), BF16),
        in_specs=[SMEM_SPEC] * 3 + [VMEM_SPEC] * 4,
        out_specs=HBM_SPEC,
        scratch_shapes=[
            pltpu.VMEM((pairs, width), F32),
            pltpu.VMEM((pairs, 3, length, width), BF16),
            pltpu.SemaphoreType.DMA((pairs,)),
        ],
        compiler_params=params(SECOND_BYTES),
        name="second_terms",
    )(slot, lead, mate, logits, target, dq, dkv)


def first_kernel(first_ref, logits_ref, target_ref, dq_ref, dkv_ref, own_ref, scale_ref):
    pairs = dq_ref.shape[0]
    scale_ref[...] = grad_scale(logits_ref[...], target_ref[...])
    own_ref[...] = jnp.zeros_like(own_ref)

    def step(p, carry):
        a = first_ref[p]
        scale = scale_ref[pl.ds(p, 1), :]
        for c in range(3):
            own_ref[a, c] += scale * (dq_ref[p] if c == 0 else dkv_ref[p, c - 1]).astype(F32)
        return carry

    lax.fori_loop(0, pairs, step, 0)


def first_terms(first, logits, target, dq, dkv, mols):
    pairs, length, width = dq.shape
    return pl.pallas_call(
        first_kernel,
        out_shape=jax.ShapeDtypeStruct((mols, 3, length, width), F32),
        in_specs=[SMEM_SPEC] + [VMEM_SPEC] * 4,
        out_specs=VMEM_SPEC,
        scratch_shapes=[pltpu.VMEM((pairs, width), F32)],
        compiler_params=params(),
        name="first_terms",
    )(first, logits, target, dq, dkv)


def finish_kernel(code_ref, own_ref, back_ref, out_ref, sum_ref):
    slots = back_ref.shape[0]
    c = pl.program_id(0)
    sum_ref[...] = own_ref[:, c]

    def step(s, carry):
        m = code_ref[s]

        @pl.when(m >= 0)
        def add():
            sum_ref[jnp.maximum(m, 0)] += back_ref[s, 0].astype(F32)

        return carry

    lax.fori_loop(0, slots, step, 0)
    out_ref[:, 0] = sum_ref[...].astype(BF16)


def finish(code, own, back):
    mols, parts, length, width = own.shape
    part = lambda i: (0, i, 0, 0)
    return pl.pallas_call(
        finish_kernel,
        grid=(parts,),
        out_shape=jax.ShapeDtypeStruct(own.shape, BF16),
        in_specs=[SMEM_SPEC, VMEM_SPEC, pl.BlockSpec((back.shape[0], 1, length, width), part)],
        out_specs=pl.BlockSpec((mols, 1, length, width), part),
        scratch_shapes=[pltpu.VMEM((mols, length, width), F32)],
        compiler_params=params(FINISH_BYTES),
        name="finish_parts",
    )(code, own, back)


def hop(value, axis, size, change):
    return lax.ppermute(value, axis, [(i, change(i)) for i in range(size)])


def sum_quarter(value, recv):
    near, far, last = recv
    return (value + far) + (near + last)


def quarters(value, size):
    quarter = size // 4
    return [hop(value, "fsdp", size, lambda i: (i + k * quarter) % size) for k in (1, 2, 3)]


def sum_shards(value, size):
    step = 1
    while step < size // 4:
        value = value + hop(value, "fsdp", size, lambda i: i ^ step)
        step *= 2
    return sum_quarter(value, quarters(value, size))


def sum_shards_beside(value, size, first_work, second_work):
    step = 1
    while step < size // 8:
        value = value + hop(value, "fsdp", size, lambda i: i ^ step)
        step *= 2
    recv = hop(value, "fsdp", size, lambda i: i ^ step)
    done = first_work(value)
    recv, done = lax.optimization_barrier((recv, done))
    value = value + recv
    recv = quarters(value, size)
    more = second_work(value)
    recv, more = lax.optimization_barrier((recv, more))
    return sum_quarter(value, recv), done, more


def turn_groups(value, groups, shards):
    where = [(g * shards + f, (g ^ f) * shards + f) for g in range(groups) for f in range(shards)]
    return lax.ppermute(value, ("group", "fsdp"), where)


def exchange(value):
    return lax.all_to_all(value, "group", split_axis=0, concat_axis=0, tiled=True)


def local(mol_qkv, pair_list, head_proj, head_out, labels):
    groups = lax.axis_size("group")
    shards = lax.axis_size("fsdp")
    device = lax.axis_index("group")
    mols = mol_qkv.shape[0]
    total_pairs = pair_list.shape[0]
    pairs = total_pairs // groups
    mol = jnp.transpose(mol_qkv, (0, 2, 1, 3))

    blocks = pair_list.T.reshape(3, groups, pairs)
    code = jnp.max(jnp.where(blocks[1] == device, blocks[2], -1), axis=1)
    mine = lax.dynamic_index_in_dim(blocks, device, 1, keepdims=False)
    first, slot = mine[0], mine[1]
    place = jnp.arange(pairs, dtype=jnp.int32)
    same = slot[:, None] == slot[None, :]
    lead = jnp.logical_not(jnp.any(same & (place[None, :] < place[:, None]), axis=1)).astype(jnp.int32)
    mate = jnp.max(jnp.where(same & (place[None, :] > place[:, None]), place[None, :], -1), axis=1)
    targets = labels.astype(F32)
    target_wide = jnp.broadcast_to(targets[:, None], (pairs, 128))

    inc = exchange(pick(code, mol))
    inc, lead, mate, target_wide = lax.optimization_barrier((inc, lead, mate, target_wide))
    part, weights, dhidden = forward(first, slot, mol, inc, head_proj, head_out)

    def grads(direction):
        def work(after):
            index, _ = lax.optimization_barrier((first, after))
            return backward(direction, index, slot, mol, inc, head_proj, weights, dhidden)

        return work

    logits_wide, (dq_b, dkv_a), (dq_a, dkv_b) = sum_shards_beside(part, shards, grads(1), grads(0))

    loss_wide = jax.nn.softplus(logits_wide) - target_wide * logits_wide
    loss_moved = turn_groups(loss_wide, groups, shards)
    out = second_terms(slot, lead, mate, logits_wide, target_wide, dq_b, dkv_b, groups)
    out, loss_moved = lax.optimization_barrier((out, loss_moved))
    back = exchange(out)
    own = first_terms(first, logits_wide, target_wide, dq_a, dkv_a, mols)
    loss_sum = jnp.sum(sum_shards(loss_moved, shards)[:, 0])
    mean_loss = loss_sum / total_pairs
    logits = logits_wide[:, 0]
    mol_grad = jnp.transpose(finish(code, own, back), (0, 2, 1, 3))
    return (mol_grad, logits, mean_loss)


def solution(mesh):
    placed = (
        P("group", None, None, "fsdp"),
        P(),
        P("fsdp", None, None),
        P("fsdp", None),
        P("group"),
    )
    return jax.shard_map(
        local,
        mesh=mesh,
        in_specs=placed,
        out_specs=(P("group", None, None, "fsdp"), P("group"), P()),
        check_vma=False,
    )
```

```python
import functools

import jax
import jax.numpy as jnp
from jax import lax
from jax.experimental import pallas as pl
from jax.experimental.pallas import tpu as pltpu
from jax.sharding import PartitionSpec as P

loss_scale = 8192.0
VMEM_BYTES = 24 * 1024 * 1024
LOSS_ROWS = 16
FINISH_BYTES = 48 * 1024 * 1024
SECOND_BYTES = 40 * 1024 * 1024
VMEM_ALL = 60 * 1024 * 1024
F32 = jnp.float32
BF16 = jnp.bfloat16
SMEM_SPEC = pl.BlockSpec(memory_space=pltpu.SMEM)
VMEM_SPEC = pl.BlockSpec(memory_space=pltpu.VMEM)
ANY_SPEC = pl.BlockSpec(memory_space=pl.ANY)


def params(limit=VMEM_BYTES):
    return pltpu.CompilerParams(vmem_limit_bytes=limit)


def mm(a, b, ca, cb):
    return lax.dot_general(a, b, (((ca,), (cb,)), ((), ())), preferred_element_type=F32)

HBM_SPEC = pl.BlockSpec(memory_space=pltpu.HBM)


def pick_kernel(pairs_ref, mol_ref, out_ref, hold_ref, in_sems, out_sems):
    slots = out_ref.shape[0]
    mols = mol_ref.shape[0]
    per_owner = pairs_ref.shape[1] // slots
    here = lax.axis_index("group")
    loads = [pltpu.make_async_copy(mol_ref.at[m], hold_ref.at[m], in_sems.at[m]) for m in range(mols)]
    for c in loads:
        c.start()
    members = []
    for s in range(slots):
        member = jnp.int32(0)
        for p in range(s * per_owner, (s + 1) * per_owner):
            member = jnp.where(pairs_ref[1, p] == here, pairs_ref[2, p], member)
        members.append(member)
    for m in range(mols):
        loads[m].wait()
        for s in range(slots):

            @pl.when(members[s] == m)
            def send():
                pltpu.make_async_copy(hold_ref.at[m], out_ref.at[s], out_sems.at[s]).start()

    for s in range(slots):
        pltpu.make_async_copy(hold_ref.at[members[s]], out_ref.at[s], out_sems.at[s]).wait()


def pick(pairs, mol, slots):
    return pl.pallas_call(
        pick_kernel,
        out_shape=jax.ShapeDtypeStruct((slots,) + mol.shape[1:], mol.dtype),
        in_specs=[SMEM_SPEC, HBM_SPEC],
        out_specs=HBM_SPEC,
        scratch_shapes=[
            pltpu.VMEM(mol.shape, mol.dtype),
            pltpu.SemaphoreType.DMA((mol.shape[0],)),
            pltpu.SemaphoreType.DMA((slots,)),
        ],
        compiler_params=params(VMEM_ALL),
        name="pick_rows",
    )(pairs, mol)


def load_units(ids, first_ref, slot_ref, mol_ref, inc_ref, heads, hd, directions):
    units = []
    for h in range(heads):
        cols = slice(h * hd, (h + 1) * hd)
        for j, p in enumerate(ids):
            a, s = first_ref[p], slot_ref[p]
            for d in directions:
                if d == 0:
                    rows = (mol_ref[a, 0, :, cols], inc_ref[s, 1, :, cols], inc_ref[s, 2, :, cols])
                else:
                    rows = (inc_ref[s, 0, :, cols], mol_ref[a, 1, :, cols], mol_ref[a, 2, :, cols])
                units.append((j, d, h) + rows)
    return units


def forward_kernel(group, first_ref, slot_ref, mol_ref, inc_ref, proj_ref, readout_ref, lp_ref, w_ref, dh_ref):
    pairs = lp_ref.shape[0]
    length = mol_ref.shape[2]
    heads, hd, _ = proj_ref.shape
    inv_root = hd ** (-0.5)
    readouts = [readout_ref[h : h + 1, :] * (1.0 / length) for h in range(heads)]

    def step(i, carry):
        ids = [i * group + j for j in range(group)]
        units = load_units(ids, first_ref, slot_ref, mol_ref, inc_ref, heads, hd, (0, 1))
        scores = [mm(u[4], u[3], 1, 1) for u in units]
        weights = []
        for sc in scores:
            lifted = jnp.exp((sc - jnp.max(sc, axis=0, keepdims=True)) * inv_root)
            weights.append(lifted * (1.0 / jnp.sum(lifted, axis=0, keepdims=True)))
        context = [mm(w.astype(BF16), u[5], 0, 0).astype(BF16) for w, u in zip(weights, units)]
        count = len(units) // heads
        totals = [None] * group
        dhidden = []
        for h in range(heads):
            hidden = mm(jnp.concatenate(context[h * count : (h + 1) * count], axis=0), proj_ref[h], 1, 0)
            sig = 0.5 + 0.5 * jnp.tanh(0.5 * hidden)
            act = hidden * sig
            for j in range(group):
                rows = jnp.sum(act[2 * j * length : (2 * j + 2) * length], axis=0, keepdims=True) * readouts[h]
                totals[j] = rows if totals[j] is None else totals[j] + rows
            dhidden.append(((sig + act * (1.0 - sig)) * readouts[h]).astype(BF16))
        for j, p in enumerate(ids):
            total = jnp.sum(totals[j], axis=1, keepdims=True)
            lp_ref[pl.ds(p, 1), :] = jnp.broadcast_to(total, (1, lp_ref.shape[1]))
        for n, (j, d, h, *_) in enumerate(units):
            at = n - h * count
            w_ref[d, ids[j], h] = weights[n]
            dh_ref[d, ids[j], h] = dhidden[h][at * length : (at + 1) * length]
        return carry

    lax.fori_loop(0, pairs // group, step, 0)


def forward(first, slot, mol, inc, proj, readout):
    pairs = first.shape[0]
    length = mol.shape[2]
    heads, _, width = proj.shape
    return pl.pallas_call(
        functools.partial(forward_kernel, min(8, pairs)),
        out_shape=(
            jax.ShapeDtypeStruct((pairs, 128), F32),
            jax.ShapeDtypeStruct((2, pairs, heads, length, length), F32),
            jax.ShapeDtypeStruct((2, pairs, heads, length, width), BF16),
        ),
        in_specs=[SMEM_SPEC] * 2 + [VMEM_SPEC] * 4,
        out_specs=(VMEM_SPEC,) * 3,
        compiler_params=params(),
        name="pair_forward",
    )(first, slot, mol, inc, proj, readout)


def backward_kernel(direction, group, first_ref, slot_ref, mol_ref, inc_ref, proj_ref, w_ref, dh_ref, dq_ref, dkv_ref):
    pairs, length, _ = dq_ref.shape
    heads, hd, _ = proj_ref.shape
    inv_root = hd ** (-0.5)

    def step(i, carry):
        ids = [i * group + j for j in range(group)]
        units = load_units(ids, first_ref, slot_ref, mol_ref, inc_ref, heads, hd, (direction,))
        weights = [w_ref[0, ids[u[0]], u[2]] for u in units]
        dcontext = []
        for h in range(heads):
            dhidden = jnp.concatenate([dh_ref[0, p, h] for p in ids], axis=0)
            whole = mm(dhidden, proj_ref[h], 1, 1).astype(BF16)
            dcontext += [whole[j * length : (j + 1) * length] for j in range(group)]
        dvalues = [mm(w.astype(BF16), dc, 1, 0).astype(BF16) for w, dc in zip(weights, dcontext)]
        dweights = [mm(u[5], dc, 1, 1) for u, dc in zip(units, dcontext)]
        dscores = []
        for w, dw in zip(weights, dweights):
            inner = jnp.sum(dw * w, axis=0, keepdims=True)
            dscores.append((w * (dw - inner) * inv_root).astype(BF16))
        dqueries = [mm(ds, u[4], 0, 0).astype(BF16) for ds, u in zip(dscores, units)]
        dkeys = [mm(ds, u[3], 1, 0).astype(BF16) for ds, u in zip(dscores, units)]
        for n, (j, _, h, *_) in enumerate(units):
            cols = slice(h * hd, (h + 1) * hd)
            dq_ref[ids[j], :, cols] = dqueries[n]
            dkv_ref[ids[j], 0, :, cols] = dkeys[n]
            dkv_ref[ids[j], 1, :, cols] = dvalues[n]
        return carry

    lax.fori_loop(0, pairs // group, step, 0)


def backward(direction, first, slot, mol, inc, proj, weights, dhidden):
    pairs = first.shape[0]
    _, parts, length, width = mol.shape
    here = lambda i: (direction, 0, 0, 0, 0)
    return pl.pallas_call(
        functools.partial(backward_kernel, direction, min(16, pairs)),
        grid=(1,),
        out_shape=(
            jax.ShapeDtypeStruct((pairs, length, width), BF16),
            jax.ShapeDtypeStruct((pairs, parts - 1, length, width), BF16),
        ),
        in_specs=[SMEM_SPEC] * 2
        + [VMEM_SPEC] * 3
        + [pl.BlockSpec((1,) + weights.shape[1:], here), pl.BlockSpec((1,) + dhidden.shape[1:], here)],
        out_specs=(VMEM_SPEC,) * 2,
        compiler_params=params(),
        name="pair_backward",
    )(first, slot, mol, inc, proj, weights, dhidden)


def grad_scale(logits, target):
    scale = (0.5 + 0.5 * jnp.tanh(0.5 * logits) - target) * loss_scale
    return jnp.concatenate([scale, scale], axis=1)


def three_parts(value):
    high = value.astype(BF16).astype(F32)
    middle = (value - high).astype(BF16).astype(F32)
    low = value - high - middle
    row = lax.broadcasted_iota(jnp.int32, (LOSS_ROWS, value.shape[1]), 0)
    rows = jnp.where(row == 0, high, jnp.where(row == 1, middle, jnp.where(row == 2, low, 0.0)))
    return rows.astype(BF16)


def second_kernel(
    slot_ref, lead_ref, mate_ref, logits_ref, target_ref, loss_ref, dq_ref, dkv_ref, out_ref, scale_ref, hold_ref, tail_ref, sems, tail_sems
):
    pairs, length, _ = dq_ref.shape
    slots = out_ref.shape[0]
    rows = 3 * length
    loss = jnp.sum(loss_ref[...], axis=0, keepdims=True)
    tail_ref[...] = three_parts(jnp.concatenate([loss, loss], axis=1))
    tails = [
        pltpu.make_async_copy(tail_ref, out_ref.at[s, pl.ds(rows, LOSS_ROWS)], tail_sems.at[s]) for s in range(slots)
    ]
    for c in tails:
        c.start()
    scale_ref[...] = grad_scale(logits_ref[...], target_ref[...])

    def send(p):
        return pltpu.make_async_copy(hold_ref.at[p], out_ref.at[slot_ref[p], pl.ds(0, rows)], sems.at[p])

    def part(p, c):
        return (dq_ref[p] if c == 0 else dkv_ref[p, c - 1]).astype(F32)

    def step(p, carry):
        mate = mate_ref[p]
        own = scale_ref[pl.ds(p, 1), :]

        @pl.when((lead_ref[p] == 1) & (mate < 0))
        def single():
            for c in range(3):
                hold_ref[p, c * length : (c + 1) * length] = (own * part(p, c)).astype(BF16)
            send(p).start()

        @pl.when((lead_ref[p] == 1) & (mate >= 0))
        def double():
            at = jnp.maximum(mate, 0)
            other = scale_ref[pl.ds(at, 1), :]
            for c in range(3):
                hold_ref[p, c * length : (c + 1) * length] = (own * part(p, c) + other * part(at, c)).astype(BF16)
            send(p).start()

        return carry

    lax.fori_loop(0, pairs, step, 0)

    def land(p, carry):
        @pl.when(lead_ref[p] == 1)
        def wait():
            send(p).wait()

        return carry

    lax.fori_loop(0, pairs, land, 0)
    for c in tails:
        c.wait()


def second_terms(slot, lead, mate, logits, target, loss, dq, dkv, slots):
    pairs, length, width = dq.shape
    return pl.pallas_call(
        second_kernel,
        out_shape=jax.ShapeDtypeStruct((slots, 3 * length + LOSS_ROWS, width), BF16),
        in_specs=[SMEM_SPEC] * 3 + [VMEM_SPEC] * 5,
        out_specs=HBM_SPEC,
        scratch_shapes=[
            pltpu.VMEM((pairs, width), F32),
            pltpu.VMEM((pairs, 3 * length, width), BF16),
            pltpu.VMEM((LOSS_ROWS, width), BF16),
            pltpu.SemaphoreType.DMA((pairs,)),
            pltpu.SemaphoreType.DMA((slots,)),
        ],
        compiler_params=params(SECOND_BYTES),
        name="second_terms",
    )(slot, lead, mate, logits, target, loss, dq, dkv)


def first_kernel(first_ref, logits_ref, target_ref, dq_ref, dkv_ref, own_ref, scale_ref):
    pairs = dq_ref.shape[0]
    scale_ref[...] = grad_scale(logits_ref[...], target_ref[...])
    own_ref[...] = jnp.zeros_like(own_ref)

    def step(p, carry):
        a = first_ref[p]
        scale = scale_ref[pl.ds(p, 1), :]
        for c in range(3):
            own_ref[a, c] += scale * (dq_ref[p] if c == 0 else dkv_ref[p, c - 1]).astype(F32)
        return carry

    lax.fori_loop(0, pairs, step, 0)


def first_terms(first, logits, target, dq, dkv, mols):
    pairs, length, width = dq.shape
    return pl.pallas_call(
        first_kernel,
        out_shape=jax.ShapeDtypeStruct((mols, 3, length, width), F32),
        in_specs=[SMEM_SPEC] + [VMEM_SPEC] * 4,
        out_specs=VMEM_SPEC,
        scratch_shapes=[pltpu.VMEM((pairs, width), F32)],
        compiler_params=params(),
        name="first_terms",
    )(first, logits, target, dq, dkv)


def finish_kernel(code_ref, own_ref, back_ref, tail_ref, out_ref, loss_ref, sum_ref):
    slots = back_ref.shape[0]
    c = pl.program_id(0)
    sum_ref[...] = own_ref[:, c]

    @pl.when(c == 0)
    def loss():
        total = tail_ref[0].astype(F32)
        for s in range(1, slots):
            total = total + tail_ref[s].astype(F32)
        loss_ref[...] = jnp.broadcast_to(jnp.sum(total, axis=0, keepdims=True)[:, :128], loss_ref.shape)

    def step(s, carry):
        m = code_ref[s]

        @pl.when(m >= 0)
        def add():
            sum_ref[jnp.maximum(m, 0)] += back_ref[s].astype(F32)

        return carry

    lax.fori_loop(0, slots, step, 0, unroll=True)
    out_ref[:, 0] = sum_ref[...].astype(BF16)


def finish(code, own, back):
    mols, parts, length, width = own.shape
    slots = back.shape[0]
    part = lambda i: (0, i, 0, 0)
    return pl.pallas_call(
        finish_kernel,
        grid=(parts,),
        out_shape=(jax.ShapeDtypeStruct(own.shape, BF16), jax.ShapeDtypeStruct((8, 128), F32)),
        in_specs=[
            SMEM_SPEC,
            VMEM_SPEC,
            pl.BlockSpec((slots, length, width), lambda i: (0, i, 0)),
            pl.BlockSpec((slots, LOSS_ROWS, width), lambda i: (0, parts * length // LOSS_ROWS, 0)),
        ],
        out_specs=(pl.BlockSpec((mols, 1, length, width), part), pl.BlockSpec((8, 128), lambda i: (0, 0))),
        scratch_shapes=[pltpu.VMEM((mols, length, width), F32)],
        compiler_params=params(FINISH_BYTES),
        name="finish_parts",
    )(code, own, back, back)


def hop(value, axis, size, change):
    return lax.ppermute(value, axis, [(i, change(i)) for i in range(size)])


def sum_quarter(value, recv):
    near, far, last = recv
    return (value + far) + (near + last)


def quarters(value, size):
    quarter = size // 4
    return [hop(value, "fsdp", size, lambda i: (i + k * quarter) % size) for k in (1, 2, 3)]


def sum_shards_beside(value, size, first_work, second_work):
    step = 1
    while step < size // 8:
        value = value + hop(value, "fsdp", size, lambda i: i ^ step)
        step *= 2
    recv = hop(value, "fsdp", size, lambda i: i ^ step)
    done = first_work(value)
    recv, done = lax.optimization_barrier((recv, done))
    value = value + recv
    recv = quarters(value, size)
    more = second_work(value)
    recv, more = lax.optimization_barrier((recv, more))
    return sum_quarter(value, recv), done, more


def exchange(value):
    return lax.all_to_all(value, "group", split_axis=0, concat_axis=0, tiled=True)


def local(mol_qkv, pair_list, head_proj, head_out, labels):
    groups = lax.axis_size("group")
    shards = lax.axis_size("fsdp")
    device = lax.axis_index("group")
    mols = mol_qkv.shape[0]
    total_pairs = pair_list.shape[0]
    pairs = total_pairs // groups
    mol = jnp.transpose(mol_qkv, (0, 2, 1, 3))

    blocks = pair_list.T.reshape(3, groups, pairs)
    code = jnp.max(jnp.where(blocks[1] == device, blocks[2], -1), axis=1)
    mine = lax.dynamic_index_in_dim(blocks, device, 1, keepdims=False)
    first, slot = mine[0], mine[1]
    place = jnp.arange(pairs, dtype=jnp.int32)
    same = slot[:, None] == slot[None, :]
    lead = jnp.logical_not(jnp.any(same & (place[None, :] < place[:, None]), axis=1)).astype(jnp.int32)
    mate = jnp.max(jnp.where(same & (place[None, :] > place[:, None]), place[None, :], -1), axis=1)
    targets = labels.astype(F32)
    target_wide = jnp.broadcast_to(targets[:, None], (pairs, 128))

    inc = exchange(pick(pair_list.T, mol, groups))
    inc, lead, mate, target_wide = lax.optimization_barrier((inc, lead, mate, target_wide))
    part, weights, dhidden = forward(first, slot, mol, inc, head_proj, head_out)

    def grads(direction):
        def work(after):
            index, _ = lax.optimization_barrier((first, after))
            return backward(direction, index, slot, mol, inc, head_proj, weights, dhidden)

        return work

    logits_wide, (dq_b, dkv_a), (dq_a, dkv_b) = sum_shards_beside(part, shards, grads(1), grads(0))

    loss_wide = jax.nn.softplus(logits_wide) - target_wide * logits_wide
    out = second_terms(slot, lead, mate, logits_wide, target_wide, loss_wide, dq_b, dkv_b, groups)
    back = exchange(out)
    own = first_terms(first, logits_wide, target_wide, dq_a, dkv_a, mols)
    logits = logits_wide[:, 0]
    grads, loss_sum = finish(code, own, back)
    mean_loss = loss_sum[0, 0] / total_pairs
    mol_grad = jnp.transpose(grads, (0, 2, 1, 3))
    return (mol_grad, logits, mean_loss)


def solution(mesh):
    placed = (
        P("group", None, None, "fsdp"),
        P(),
        P("fsdp", None, None),
        P("fsdp", None),
        P("group"),
    )
    return jax.shard_map(
        local,
        mesh=mesh,
        in_specs=placed,
        out_specs=(P("group", None, None, "fsdp"), P("group"), P()),
        check_vma=False,
    )
```

```python
import functools

import jax
import jax.numpy as jnp
from jax import lax
from jax.experimental import pallas as pl
from jax.experimental.pallas import tpu as pltpu
from jax.sharding import PartitionSpec as P

loss_scale = 8192.0
VMEM_BYTES = 24 * 1024 * 1024
LOSS_ROWS = 16
FINISH_BYTES = 48 * 1024 * 1024
SECOND_BYTES = 40 * 1024 * 1024
VMEM_ALL = 60 * 1024 * 1024
F32 = jnp.float32
BF16 = jnp.bfloat16
SMEM_SPEC = pl.BlockSpec(memory_space=pltpu.SMEM)
VMEM_SPEC = pl.BlockSpec(memory_space=pltpu.VMEM)
ANY_SPEC = pl.BlockSpec(memory_space=pl.ANY)


def params(limit=VMEM_BYTES):
    return pltpu.CompilerParams(vmem_limit_bytes=limit)


def mm(a, b, ca, cb):
    return lax.dot_general(a, b, (((ca,), (cb,)), ((), ())), preferred_element_type=F32)

HBM_SPEC = pl.BlockSpec(memory_space=pltpu.HBM)


def pick_kernel(pairs_ref, mol_ref, out_ref, hold_ref, in_sems, out_sems):
    slots = out_ref.shape[0]
    mols = mol_ref.shape[0]
    per_owner = pairs_ref.shape[1] // slots
    here = lax.axis_index("group")
    loads = [pltpu.make_async_copy(mol_ref.at[m], hold_ref.at[m], in_sems.at[m]) for m in range(mols)]
    for c in loads:
        c.start()
    members = []
    for s in range(slots):
        member = jnp.int32(0)
        for p in range(s * per_owner, (s + 1) * per_owner):
            member = jnp.where(pairs_ref[1, p] == here, pairs_ref[2, p], member)
        members.append(member)
    for m in range(mols):
        loads[m].wait()
        for s in range(slots):

            @pl.when(members[s] == m)
            def send():
                pltpu.make_async_copy(hold_ref.at[m], out_ref.at[s], out_sems.at[s]).start()

    for s in range(slots):
        pltpu.make_async_copy(hold_ref.at[members[s]], out_ref.at[s], out_sems.at[s]).wait()


def pick(pairs, mol, slots):
    return pl.pallas_call(
        pick_kernel,
        out_shape=jax.ShapeDtypeStruct((slots,) + mol.shape[1:], mol.dtype),
        in_specs=[SMEM_SPEC, HBM_SPEC],
        out_specs=HBM_SPEC,
        scratch_shapes=[
            pltpu.VMEM(mol.shape, mol.dtype),
            pltpu.SemaphoreType.DMA((mol.shape[0],)),
            pltpu.SemaphoreType.DMA((slots,)),
        ],
        compiler_params=params(VMEM_ALL),
        name="pick_rows",
    )(pairs, mol)


def load_units(ids, first_ref, slot_ref, mol_ref, inc_ref, heads, hd, directions):
    units = []
    for h in range(heads):
        cols = slice(h * hd, (h + 1) * hd)
        for j, p in enumerate(ids):
            a, s = first_ref[p], slot_ref[p]
            for d in directions:
                if d == 0:
                    rows = (mol_ref[a, 0, :, cols], inc_ref[s, 1, :, cols], inc_ref[s, 2, :, cols])
                else:
                    rows = (inc_ref[s, 0, :, cols], mol_ref[a, 1, :, cols], mol_ref[a, 2, :, cols])
                units.append((j, d, h) + rows)
    return units


def forward_kernel(group, first_ref, slot_ref, mol_ref, inc_ref, proj_ref, readout_ref, lp_ref, w_ref, dh_ref):
    pairs = lp_ref.shape[0]
    length = mol_ref.shape[2]
    heads, hd, _ = proj_ref.shape
    inv_root = hd ** (-0.5)
    readouts = [readout_ref[h : h + 1, :] * (1.0 / length) for h in range(heads)]

    def step(i, carry):
        ids = [i * group + j for j in range(group)]
        units = load_units(ids, first_ref, slot_ref, mol_ref, inc_ref, heads, hd, (0, 1))
        scores = [mm(u[4], u[3], 1, 1) for u in units]
        weights = []
        for sc in scores:
            lifted = jnp.exp((sc - jnp.max(sc, axis=0, keepdims=True)) * inv_root)
            weights.append(lifted * (1.0 / jnp.sum(lifted, axis=0, keepdims=True)))
        context = [mm(w.astype(BF16), u[5], 0, 0).astype(BF16) for w, u in zip(weights, units)]
        count = len(units) // heads
        totals = [None] * group
        dhidden = []
        for h in range(heads):
            hidden = mm(jnp.concatenate(context[h * count : (h + 1) * count], axis=0), proj_ref[h], 1, 0)
            sig = 0.5 + 0.5 * jnp.tanh(0.5 * hidden)
            act = hidden * sig
            for j in range(group):
                rows = jnp.sum(act[2 * j * length : (2 * j + 2) * length], axis=0, keepdims=True) * readouts[h]
                totals[j] = rows if totals[j] is None else totals[j] + rows
            dhidden.append(((sig + act * (1.0 - sig)) * readouts[h]).astype(BF16))
        for j, p in enumerate(ids):
            total = jnp.sum(totals[j], axis=1, keepdims=True)
            lp_ref[pl.ds(p, 1), :] = jnp.broadcast_to(total, (1, lp_ref.shape[1]))
        for n, (j, d, h, *_) in enumerate(units):
            at = n - h * count
            w_ref[d, ids[j], h] = weights[n]
            dh_ref[d, ids[j], h] = dhidden[h][at * length : (at + 1) * length]
        return carry

    lax.fori_loop(0, pairs // group, step, 0)


def forward(first, slot, mol, inc, proj, readout):
    pairs = first.shape[0]
    length = mol.shape[2]
    heads, _, width = proj.shape
    return pl.pallas_call(
        functools.partial(forward_kernel, min(16, pairs)),
        out_shape=(
            jax.ShapeDtypeStruct((pairs, 128), F32),
            jax.ShapeDtypeStruct((2, pairs, heads, length, length), F32),
            jax.ShapeDtypeStruct((2, pairs, heads, length, width), BF16),
        ),
        in_specs=[SMEM_SPEC] * 2 + [VMEM_SPEC] * 4,
        out_specs=(VMEM_SPEC,) * 3,
        compiler_params=params(),
        name="pair_forward",
    )(first, slot, mol, inc, proj, readout)


def backward_kernel(direction, group, first_ref, slot_ref, mol_ref, inc_ref, proj_ref, w_ref, dh_ref, dq_ref, dkv_ref):
    pairs, length, _ = dq_ref.shape
    heads, hd, _ = proj_ref.shape
    inv_root = hd ** (-0.5)

    def step(i, carry):
        ids = [i * group + j for j in range(group)]
        units = load_units(ids, first_ref, slot_ref, mol_ref, inc_ref, heads, hd, (direction,))
        weights = [w_ref[0, ids[u[0]], u[2]] for u in units]
        dcontext = []
        for h in range(heads):
            dhidden = jnp.concatenate([dh_ref[0, p, h] for p in ids], axis=0)
            whole = mm(dhidden, proj_ref[h], 1, 1).astype(BF16)
            dcontext += [whole[j * length : (j + 1) * length] for j in range(group)]
        dvalues = [mm(w.astype(BF16), dc, 1, 0).astype(BF16) for w, dc in zip(weights, dcontext)]
        dweights = [mm(u[5], dc, 1, 1) for u, dc in zip(units, dcontext)]
        dscores = []
        for w, dw in zip(weights, dweights):
            inner = jnp.sum(dw * w, axis=0, keepdims=True)
            dscores.append((w * (dw - inner) * inv_root).astype(BF16))
        dqueries = [mm(ds, u[4], 0, 0).astype(BF16) for ds, u in zip(dscores, units)]
        dkeys = [mm(ds, u[3], 1, 0).astype(BF16) for ds, u in zip(dscores, units)]
        for n, (j, _, h, *_) in enumerate(units):
            cols = slice(h * hd, (h + 1) * hd)
            dq_ref[ids[j], :, cols] = dqueries[n]
            dkv_ref[ids[j], 0, :, cols] = dkeys[n]
            dkv_ref[ids[j], 1, :, cols] = dvalues[n]
        return carry

    lax.fori_loop(0, pairs // group, step, 0)


def backward(direction, first, slot, mol, inc, proj, weights, dhidden):
    pairs = first.shape[0]
    _, parts, length, width = mol.shape
    here = lambda i: (direction, 0, 0, 0, 0)
    return pl.pallas_call(
        functools.partial(backward_kernel, direction, min(16, pairs)),
        grid=(1,),
        out_shape=(
            jax.ShapeDtypeStruct((pairs, length, width), BF16),
            jax.ShapeDtypeStruct((pairs, parts - 1, length, width), BF16),
        ),
        in_specs=[SMEM_SPEC] * 2
        + [VMEM_SPEC] * 3
        + [pl.BlockSpec((1,) + weights.shape[1:], here), pl.BlockSpec((1,) + dhidden.shape[1:], here)],
        out_specs=(VMEM_SPEC,) * 2,
        compiler_params=params(),
        name="pair_backward",
    )(first, slot, mol, inc, proj, weights, dhidden)


def grad_scale(logits, target):
    scale = (0.5 + 0.5 * jnp.tanh(0.5 * logits) - target) * loss_scale
    return jnp.concatenate([scale, scale], axis=1)


def three_parts(value):
    high = value.astype(BF16).astype(F32)
    middle = (value - high).astype(BF16).astype(F32)
    low = value - high - middle
    row = lax.broadcasted_iota(jnp.int32, (LOSS_ROWS, value.shape[1]), 0)
    rows = jnp.where(row == 0, high, jnp.where(row == 1, middle, jnp.where(row == 2, low, 0.0)))
    return rows.astype(BF16)


def scale_kernel(
    first_ref,
    slot_ref,
    lead_ref,
    mate_ref,
    logits_ref,
    target_ref,
    loss_ref,
    dq_ref,
    dkv_ref,
    own_dq_ref,
    own_dkv_ref,
    out_ref,
    own_ref,
    scale_ref,
    hold_ref,
    tail_ref,
    sems,
    tail_sems,
):
    pairs, length, _ = dq_ref.shape
    slots = out_ref.shape[0]
    rows = 3 * length
    loss = jnp.sum(loss_ref[...], axis=0, keepdims=True)
    tail_ref[...] = three_parts(jnp.concatenate([loss, loss], axis=1))
    tails = [
        pltpu.make_async_copy(tail_ref, out_ref.at[s, pl.ds(rows, LOSS_ROWS)], tail_sems.at[s]) for s in range(slots)
    ]
    for c in tails:
        c.start()
    scale_ref[...] = grad_scale(logits_ref[...], target_ref[...])

    def send(p):
        return pltpu.make_async_copy(hold_ref.at[p], out_ref.at[slot_ref[p], pl.ds(0, rows)], sems.at[p])

    def part(p, c):
        return (dq_ref[p] if c == 0 else dkv_ref[p, c - 1]).astype(F32)

    def step(p, carry):
        mate = mate_ref[p]
        own = scale_ref[pl.ds(p, 1), :]

        @pl.when((lead_ref[p] == 1) & (mate < 0))
        def single():
            for c in range(3):
                hold_ref[p, c * length : (c + 1) * length] = (own * part(p, c)).astype(BF16)
            send(p).start()

        @pl.when((lead_ref[p] == 1) & (mate >= 0))
        def double():
            at = jnp.maximum(mate, 0)
            other = scale_ref[pl.ds(at, 1), :]
            for c in range(3):
                hold_ref[p, c * length : (c + 1) * length] = (own * part(p, c) + other * part(at, c)).astype(BF16)
            send(p).start()

        return carry

    lax.fori_loop(0, pairs, step, 0)
    own_ref[...] = jnp.zeros_like(own_ref)

    def own_step(p, carry):
        a = first_ref[p]
        scale = scale_ref[pl.ds(p, 1), :]
        for c in range(3):
            own_ref[a, c] += scale * (own_dq_ref[p] if c == 0 else own_dkv_ref[p, c - 1]).astype(F32)
        return carry

    lax.fori_loop(0, pairs, own_step, 0)

    def land(p, carry):
        @pl.when(lead_ref[p] == 1)
        def wait():
            send(p).wait()

        return carry

    lax.fori_loop(0, pairs, land, 0)
    for c in tails:
        c.wait()


def scaled_terms(first, slot, lead, mate, logits, target, loss, second, own, slots, mols):
    pairs, length, width = second[0].shape
    return pl.pallas_call(
        scale_kernel,
        out_shape=(
            jax.ShapeDtypeStruct((slots, 3 * length + LOSS_ROWS, width), BF16),
            jax.ShapeDtypeStruct((mols, 3, length, width), F32),
        ),
        in_specs=[SMEM_SPEC] * 4 + [VMEM_SPEC] * 7,
        out_specs=(HBM_SPEC, VMEM_SPEC),
        scratch_shapes=[
            pltpu.VMEM((pairs, width), F32),
            pltpu.VMEM((pairs, 3 * length, width), BF16),
            pltpu.VMEM((LOSS_ROWS, width), BF16),
            pltpu.SemaphoreType.DMA((pairs,)),
            pltpu.SemaphoreType.DMA((slots,)),
        ],
        compiler_params=params(SECOND_BYTES),
        name="scaled_terms",
    )(first, slot, lead, mate, logits, target, loss, *second, *own)


def finish_kernel(scale, code_ref, own_ref, back_ref, out_ref, loss_ref, held_ref, tail_ref, sum_ref, done_ref, sems, tail_sem, out_sems):
    slots = back_ref.shape[0]
    mols, parts, length, _ = own_ref.shape
    codes = [code_ref[s] for s in range(slots)]

    def load(c, s):
        rows = pl.ds(c * length, length)
        return pltpu.make_async_copy(back_ref.at[s, rows], held_ref.at[s, rows], sems.at[c, s])

    for c in range(parts):
        for s in range(slots):
            pl.when(codes[s] >= 0)(load(c, s).start)
    tail = pltpu.make_async_copy(back_ref.at[:, pl.ds(parts * length, LOSS_ROWS)], tail_ref, tail_sem)
    tail.start()

    for c in range(parts):
        sum_ref[...] = own_ref[:, c]
        for s in range(slots):

            @pl.when(codes[s] >= 0)
            def add():
                load(c, s).wait()
                sum_ref[jnp.maximum(codes[s], 0)] += held_ref[s, c * length : (c + 1) * length].astype(F32)

        done_ref[c] = sum_ref[...].astype(BF16)
        pltpu.make_async_copy(done_ref.at[c], out_ref.at[:, c], out_sems.at[c]).start()

    tail.wait()
    total = tail_ref[0].astype(F32)
    for s in range(1, slots):
        total = total + tail_ref[s].astype(F32)
    loss_ref[0, 0] = jnp.sum(total[:, :1]) * scale
    for c in range(parts):
        pltpu.make_async_copy(done_ref.at[c], out_ref.at[:, c], out_sems.at[c]).wait()


def finish(code, own, back, scale):
    mols, parts, length, width = own.shape
    slots = back.shape[0]
    return pl.pallas_call(
        functools.partial(finish_kernel, scale),
        out_shape=(jax.ShapeDtypeStruct(own.shape, BF16), jax.ShapeDtypeStruct((1, 1), F32)),
        in_specs=[SMEM_SPEC, VMEM_SPEC, HBM_SPEC],
        out_specs=(HBM_SPEC, SMEM_SPEC),
        scratch_shapes=[
            pltpu.VMEM((slots, parts * length, width), BF16),
            pltpu.VMEM((slots, LOSS_ROWS, width), BF16),
            pltpu.VMEM((mols, length, width), F32),
            pltpu.VMEM((parts, mols, length, width), BF16),
            pltpu.SemaphoreType.DMA((parts, slots)),
            pltpu.SemaphoreType.DMA,
            pltpu.SemaphoreType.DMA((parts,)),
        ],
        compiler_params=params(FINISH_BYTES),
        name="finish_parts",
    )(code, own, back)


def hop(value, axis, size, change):
    return lax.ppermute(value, axis, [(i, change(i)) for i in range(size)])


def sum_quarter(value, recv):
    near, far, last = recv
    return (value + far) + (near + last)


def quarters(value, size):
    quarter = size // 4
    return [hop(value, "fsdp", size, lambda i: (i + k * quarter) % size) for k in (1, 2, 3)]


def sum_shards_beside(value, size, first_work, second_work):
    step = 1
    while step < size // 8:
        value = value + hop(value, "fsdp", size, lambda i: i ^ step)
        step *= 2
    recv = hop(value, "fsdp", size, lambda i: i ^ step)
    done = first_work(value)
    recv, done = lax.optimization_barrier((recv, done))
    value = value + recv
    recv = quarters(value, size)
    more = second_work(value)
    recv, more = lax.optimization_barrier((recv, more))
    return sum_quarter(value, recv), done, more


def exchange(value):
    return lax.all_to_all(value, "group", split_axis=0, concat_axis=0, tiled=True)


def local(mol_qkv, pair_list, head_proj, head_out, labels):
    groups = lax.axis_size("group")
    shards = lax.axis_size("fsdp")
    device = lax.axis_index("group")
    mols = mol_qkv.shape[0]
    total_pairs = pair_list.shape[0]
    pairs = total_pairs // groups
    mol = jnp.transpose(mol_qkv, (0, 2, 1, 3))

    blocks = pair_list.T.reshape(3, groups, pairs)
    code = jnp.max(jnp.where(blocks[1] == device, blocks[2], -1), axis=1)
    mine = lax.dynamic_index_in_dim(blocks, device, 1, keepdims=False)
    first, slot = mine[0], mine[1]
    place = jnp.arange(pairs, dtype=jnp.int32)
    same = slot[:, None] == slot[None, :]
    lead = jnp.logical_not(jnp.any(same & (place[None, :] < place[:, None]), axis=1)).astype(jnp.int32)
    mate = jnp.max(jnp.where(same & (place[None, :] > place[:, None]), place[None, :], -1), axis=1)
    targets = labels.astype(F32)
    target_wide = jnp.broadcast_to(targets[:, None], (pairs, 128))

    inc = exchange(pick(pair_list.T, mol, groups))
    inc, lead, mate, target_wide = lax.optimization_barrier((inc, lead, mate, target_wide))
    part, weights, dhidden = forward(first, slot, mol, inc, head_proj, head_out)

    def grads(direction):
        def work(after):
            index, _ = lax.optimization_barrier((first, after))
            return backward(direction, index, slot, mol, inc, head_proj, weights, dhidden)

        return work

    logits_wide, (dq_b, dkv_a), (dq_a, dkv_b) = sum_shards_beside(part, shards, grads(1), grads(0))

    loss_wide = jax.nn.softplus(logits_wide) - target_wide * logits_wide
    out, own = scaled_terms(
        first, slot, lead, mate, logits_wide, target_wide, loss_wide, (dq_b, dkv_b), (dq_a, dkv_a), groups, mols
    )
    back = exchange(out)
    logits = logits_wide[:, 0]
    grads, mean_loss = finish(code, own, back, 1.0 / total_pairs)
    mean_loss = mean_loss.reshape(())
    mol_grad = jnp.transpose(grads, (0, 2, 1, 3))
    return (mol_grad, logits, mean_loss)


def solution(mesh):
    placed = (
        P("group", None, None, "fsdp"),
        P(),
        P("fsdp", None, None),
        P("fsdp", None),
        P("group"),
    )
    return jax.shard_map(
        local,
        mesh=mesh,
        in_specs=placed,
        out_specs=(P("group", None, None, "fsdp"), P("group"), P()),
        check_vma=False,
    )
```

```python
import functools

import jax
import jax.numpy as jnp
from jax import lax
from jax.experimental import pallas as pl
from jax.experimental.pallas import tpu as pltpu
from jax.sharding import PartitionSpec as P

loss_scale = 8192.0
VMEM_BYTES = 24 * 1024 * 1024
LOSS_ROWS = 16
FINISH_BYTES = 48 * 1024 * 1024
SECOND_BYTES = 40 * 1024 * 1024
VMEM_ALL = 60 * 1024 * 1024
F32 = jnp.float32
BF16 = jnp.bfloat16
SMEM_SPEC = pl.BlockSpec(memory_space=pltpu.SMEM)
VMEM_SPEC = pl.BlockSpec(memory_space=pltpu.VMEM)
ANY_SPEC = pl.BlockSpec(memory_space=pl.ANY)


def params(limit=VMEM_BYTES):
    return pltpu.CompilerParams(vmem_limit_bytes=limit)


def mm(a, b, ca, cb):
    return lax.dot_general(a, b, (((ca,), (cb,)), ((), ())), preferred_element_type=F32)

HBM_SPEC = pl.BlockSpec(memory_space=pltpu.HBM)


def pick_kernel(pairs_ref, mol_ref, out_ref, hold_ref, in_sems, out_sems):
    slots = out_ref.shape[0]
    mols = mol_ref.shape[0]
    per_owner = pairs_ref.shape[1] // slots
    here = lax.axis_index("group")
    loads = [pltpu.make_async_copy(mol_ref.at[m], hold_ref.at[m], in_sems.at[m]) for m in range(mols)]
    for c in loads:
        c.start()
    members = []
    for s in range(slots):
        member = jnp.int32(0)
        for p in range(s * per_owner, (s + 1) * per_owner):
            member = jnp.where(pairs_ref[1, p] == here, pairs_ref[2, p], member)
        members.append(member)
    for m in range(mols):
        loads[m].wait()
        for s in range(slots):

            @pl.when(members[s] == m)
            def send():
                pltpu.make_async_copy(hold_ref.at[m], out_ref.at[s], out_sems.at[s]).start()

    for s in range(slots):
        pltpu.make_async_copy(hold_ref.at[members[s]], out_ref.at[s], out_sems.at[s]).wait()


def pick(pairs, mol, slots):
    return pl.pallas_call(
        pick_kernel,
        out_shape=jax.ShapeDtypeStruct((slots,) + mol.shape[1:], mol.dtype),
        in_specs=[SMEM_SPEC, HBM_SPEC],
        out_specs=HBM_SPEC,
        scratch_shapes=[
            pltpu.VMEM(mol.shape, mol.dtype),
            pltpu.SemaphoreType.DMA((mol.shape[0],)),
            pltpu.SemaphoreType.DMA((slots,)),
        ],
        compiler_params=params(VMEM_ALL),
        name="pick_rows",
    )(pairs, mol)


def load_units(ids, first_ref, slot_ref, mol_ref, inc_ref, heads, hd, directions):
    units = []
    for h in range(heads):
        cols = slice(h * hd, (h + 1) * hd)
        for j, p in enumerate(ids):
            a, s = first_ref[p], slot_ref[p]
            for d in directions:
                if d == 0:
                    rows = (mol_ref[a, 0, :, cols], inc_ref[s, 1, :, cols], inc_ref[s, 2, :, cols])
                else:
                    rows = (inc_ref[s, 0, :, cols], mol_ref[a, 1, :, cols], mol_ref[a, 2, :, cols])
                units.append((j, d, h) + rows)
    return units


def forward_kernel(group, first_ref, slot_ref, mol_ref, inc_ref, proj_ref, readout_ref, lp_ref, w_ref, dh_ref):
    pairs = lp_ref.shape[0]
    length = mol_ref.shape[2]
    heads, hd, _ = proj_ref.shape
    inv_root = hd ** (-0.5)
    readouts = [readout_ref[h : h + 1, :] * (1.0 / length) for h in range(heads)]

    def step(i, carry):
        ids = [i * group + j for j in range(group)]
        units = load_units(ids, first_ref, slot_ref, mol_ref, inc_ref, heads, hd, (0, 1))
        scores = [mm(u[4], u[3], 1, 1) for u in units]
        weights = []
        for sc in scores:
            lifted = jnp.exp((sc - jnp.max(sc, axis=0, keepdims=True)) * inv_root)
            weights.append(lifted * (1.0 / jnp.sum(lifted, axis=0, keepdims=True)))
        context = [mm(w.astype(BF16), u[5], 0, 0).astype(BF16) for w, u in zip(weights, units)]
        count = len(units) // heads
        totals = [None] * group
        dhidden = []
        for h in range(heads):
            hidden = mm(jnp.concatenate(context[h * count : (h + 1) * count], axis=0), proj_ref[h], 1, 0)
            sig = 0.5 + 0.5 * jnp.tanh(0.5 * hidden)
            act = hidden * sig
            for j in range(group):
                rows = jnp.sum(act[2 * j * length : (2 * j + 2) * length], axis=0, keepdims=True) * readouts[h]
                totals[j] = rows if totals[j] is None else totals[j] + rows
            dhidden.append(((sig + act * (1.0 - sig)) * readouts[h]).astype(BF16))
        for j, p in enumerate(ids):
            total = jnp.sum(totals[j], axis=1, keepdims=True)
            lp_ref[pl.ds(p, 1), :] = jnp.broadcast_to(total, (1, lp_ref.shape[1]))
        for n, (j, d, h, *_) in enumerate(units):
            at = n - h * count
            w_ref[d, ids[j], h] = weights[n]
            dh_ref[d, ids[j], h] = dhidden[h][at * length : (at + 1) * length]
        return carry

    lax.fori_loop(0, pairs // group, step, 0)


def forward(first, slot, mol, inc, proj, readout):
    pairs = first.shape[0]
    length = mol.shape[2]
    heads, _, width = proj.shape
    return pl.pallas_call(
        functools.partial(forward_kernel, min(16, pairs)),
        out_shape=(
            jax.ShapeDtypeStruct((pairs, 128), F32),
            jax.ShapeDtypeStruct((2, pairs, heads, length, length), F32),
            jax.ShapeDtypeStruct((2, pairs, heads, length, width), BF16),
        ),
        in_specs=[SMEM_SPEC] * 2 + [VMEM_SPEC] * 4,
        out_specs=(VMEM_SPEC,) * 3,
        compiler_params=params(),
        name="pair_forward",
    )(first, slot, mol, inc, proj, readout)


def backward_kernel(direction, group, first_ref, slot_ref, mol_ref, inc_ref, proj_ref, w_ref, dh_ref, dq_ref, dkv_ref):
    pairs, length, _ = dq_ref.shape
    heads, hd, _ = proj_ref.shape
    inv_root = hd ** (-0.5)

    def step(i, carry):
        ids = [i * group + j for j in range(group)]
        units = load_units(ids, first_ref, slot_ref, mol_ref, inc_ref, heads, hd, (direction,))
        weights = [w_ref[0, ids[u[0]], u[2]] for u in units]
        dcontext = []
        for h in range(heads):
            dhidden = jnp.concatenate([dh_ref[0, p, h] for p in ids], axis=0)
            whole = mm(dhidden, proj_ref[h], 1, 1).astype(BF16)
            dcontext += [whole[j * length : (j + 1) * length] for j in range(group)]
        dvalues = [mm(w.astype(BF16), dc, 1, 0).astype(BF16) for w, dc in zip(weights, dcontext)]
        dweights = [mm(u[5], dc, 1, 1) for u, dc in zip(units, dcontext)]
        dscores = []
        for w, dw in zip(weights, dweights):
            inner = jnp.sum(dw * w, axis=0, keepdims=True)
            dscores.append((w * (dw - inner) * inv_root).astype(BF16))
        dqueries = [mm(ds, u[4], 0, 0).astype(BF16) for ds, u in zip(dscores, units)]
        dkeys = [mm(ds, u[3], 1, 0).astype(BF16) for ds, u in zip(dscores, units)]
        for n, (j, _, h, *_) in enumerate(units):
            cols = slice(h * hd, (h + 1) * hd)
            dq_ref[ids[j], :, cols] = dqueries[n]
            dkv_ref[ids[j], 0, :, cols] = dkeys[n]
            dkv_ref[ids[j], 1, :, cols] = dvalues[n]
        return carry

    lax.fori_loop(0, pairs // group, step, 0)


def backward(direction, first, slot, mol, inc, proj, weights, dhidden):
    pairs = first.shape[0]
    _, parts, length, width = mol.shape
    here = lambda i: (direction, 0, 0, 0, 0)
    return pl.pallas_call(
        functools.partial(backward_kernel, direction, min(16, pairs)),
        grid=(1,),
        out_shape=(
            jax.ShapeDtypeStruct((pairs, length, width), BF16),
            jax.ShapeDtypeStruct((pairs, parts - 1, length, width), BF16),
        ),
        in_specs=[SMEM_SPEC] * 2
        + [VMEM_SPEC] * 3
        + [pl.BlockSpec((1,) + weights.shape[1:], here), pl.BlockSpec((1,) + dhidden.shape[1:], here)],
        out_specs=(VMEM_SPEC,) * 2,
        compiler_params=params(),
        name="pair_backward",
    )(first, slot, mol, inc, proj, weights, dhidden)


def grad_scale(logits, target):
    scale = (0.5 + 0.5 * jnp.tanh(0.5 * logits) - target) * loss_scale
    return jnp.concatenate([scale, scale], axis=1)


def three_parts(value):
    high = value.astype(BF16).astype(F32)
    middle = (value - high).astype(BF16).astype(F32)
    low = value - high - middle
    row = lax.broadcasted_iota(jnp.int32, (LOSS_ROWS, value.shape[1]), 0)
    rows = jnp.where(row == 0, high, jnp.where(row == 1, middle, jnp.where(row == 2, low, 0.0)))
    return rows.astype(BF16)


def scale_kernel(
    first_ref,
    slot_ref,
    lead_ref,
    mate_ref,
    logits_ref,
    target_ref,
    loss_ref,
    dq_ref,
    dkv_ref,
    own_dq_ref,
    own_dkv_ref,
    out_ref,
    own_ref,
    scale_ref,
    hold_ref,
    tail_ref,
    sems,
    tail_sems,
):
    pairs, length, width = dq_ref.shape
    slots, _, hd = out_ref.shape
    heads = width // hd
    rows = 3 * heads * length
    tail_ref[...] = three_parts(jnp.sum(loss_ref[...], axis=0, keepdims=True))
    tails = [
        pltpu.make_async_copy(tail_ref, out_ref.at[s, pl.ds(rows, LOSS_ROWS)], tail_sems.at[s]) for s in range(slots)
    ]
    for c in tails:
        c.start()
    scale_ref[...] = grad_scale(logits_ref[...], target_ref[...])

    def send(p):
        return pltpu.make_async_copy(hold_ref.at[p], out_ref.at[slot_ref[p], pl.ds(0, rows)], sems.at[p])

    def part(p, c):
        return (dq_ref[p] if c == 0 else dkv_ref[p, c - 1]).astype(F32)

    def hold(p, c, value):
        value = value.astype(BF16)
        for h in range(heads):
            at = (c * heads + h) * length
            hold_ref[p, at : at + length] = value[:, h * hd : (h + 1) * hd]

    def step(p, carry):
        mate = mate_ref[p]
        own = scale_ref[pl.ds(p, 1), :]

        @pl.when((lead_ref[p] == 1) & (mate < 0))
        def single():
            for c in range(3):
                hold(p, c, own * part(p, c))
            send(p).start()

        @pl.when((lead_ref[p] == 1) & (mate >= 0))
        def double():
            at = jnp.maximum(mate, 0)
            other = scale_ref[pl.ds(at, 1), :]
            for c in range(3):
                hold(p, c, own * part(p, c) + other * part(at, c))
            send(p).start()

        return carry

    lax.fori_loop(0, pairs, step, 0)
    own_ref[...] = jnp.zeros_like(own_ref)

    def own_step(p, carry):
        a = first_ref[p]
        scale = scale_ref[pl.ds(p, 1), :]
        for c in range(3):
            own_ref[a, c] += scale * (own_dq_ref[p] if c == 0 else own_dkv_ref[p, c - 1]).astype(F32)
        return carry

    lax.fori_loop(0, pairs, own_step, 0)

    def land(p, carry):
        @pl.when(lead_ref[p] == 1)
        def wait():
            send(p).wait()

        return carry

    lax.fori_loop(0, pairs, land, 0)
    for c in tails:
        c.wait()


def scaled_terms(first, slot, lead, mate, logits, target, loss, second, own, slots, mols):
    pairs, length, width = second[0].shape
    hd = logits.shape[1]
    rows = 3 * length * (width // hd)
    return pl.pallas_call(
        scale_kernel,
        out_shape=(
            jax.ShapeDtypeStruct((slots, rows + LOSS_ROWS, hd), BF16),
            jax.ShapeDtypeStruct((mols, 3, length, width), F32),
        ),
        in_specs=[SMEM_SPEC] * 4 + [VMEM_SPEC] * 7,
        out_specs=(HBM_SPEC, VMEM_SPEC),
        scratch_shapes=[
            pltpu.VMEM((pairs, width), F32),
            pltpu.VMEM((pairs, rows, hd), BF16),
            pltpu.VMEM((LOSS_ROWS, hd), BF16),
            pltpu.SemaphoreType.DMA((pairs,)),
            pltpu.SemaphoreType.DMA((slots,)),
        ],
        compiler_params=params(SECOND_BYTES),
        name="scaled_terms",
    )(first, slot, lead, mate, logits, target, loss, *second, *own)


def finish_kernel(scale, code_ref, own_ref, back_ref, out_ref, loss_ref, held_ref, tail_ref, sum_ref, done_ref, sems, tail_sem, out_sems):
    slots, _, hd = back_ref.shape
    mols, parts, length, width = own_ref.shape
    heads = width // hd
    block = heads * length
    codes = [code_ref[s] for s in range(slots)]

    def load(c, s):
        rows = pl.ds(c * block, block)
        return pltpu.make_async_copy(back_ref.at[s, rows], held_ref.at[s, rows], sems.at[c, s])

    for c in range(parts):
        for s in range(slots):
            pl.when(codes[s] >= 0)(load(c, s).start)
    tail = pltpu.make_async_copy(back_ref.at[:, pl.ds(parts * block, LOSS_ROWS)], tail_ref, tail_sem)
    tail.start()

    for c in range(parts):
        sum_ref[...] = own_ref[:, c]
        for s in range(slots):

            @pl.when(codes[s] >= 0)
            def add():
                load(c, s).wait()
                for h in range(heads):
                    at = c * block + h * length
                    cols = slice(h * hd, (h + 1) * hd)
                    sum_ref[jnp.maximum(codes[s], 0), :, cols] += held_ref[s, at : at + length].astype(F32)

        done_ref[c] = sum_ref[...].astype(BF16)
        pltpu.make_async_copy(done_ref.at[c], out_ref.at[:, c], out_sems.at[c]).start()

    tail.wait()
    total = tail_ref[0].astype(F32)
    for s in range(1, slots):
        total = total + tail_ref[s].astype(F32)
    loss_ref[0, 0] = jnp.sum(total[:, :1]) * scale
    for c in range(parts):
        pltpu.make_async_copy(done_ref.at[c], out_ref.at[:, c], out_sems.at[c]).wait()


def finish(code, own, back, scale):
    mols, parts, length, width = own.shape
    slots, rows, hd = back.shape
    return pl.pallas_call(
        functools.partial(finish_kernel, scale),
        out_shape=(jax.ShapeDtypeStruct(own.shape, BF16), jax.ShapeDtypeStruct((1, 1), F32)),
        in_specs=[SMEM_SPEC, VMEM_SPEC, HBM_SPEC],
        out_specs=(HBM_SPEC, SMEM_SPEC),
        scratch_shapes=[
            pltpu.VMEM((slots, rows - LOSS_ROWS, hd), BF16),
            pltpu.VMEM((slots, LOSS_ROWS, hd), BF16),
            pltpu.VMEM((mols, length, width), F32),
            pltpu.VMEM((parts, mols, length, width), BF16),
            pltpu.SemaphoreType.DMA((parts, slots)),
            pltpu.SemaphoreType.DMA,
            pltpu.SemaphoreType.DMA((parts,)),
        ],
        compiler_params=params(FINISH_BYTES),
        name="finish_parts",
    )(code, own, back)


def hop(value, axis, size, change):
    return lax.ppermute(value, axis, [(i, change(i)) for i in range(size)])


def sum_quarter(value, recv):
    near, far, last = recv
    return (value + far) + (near + last)


def quarters(value, size):
    quarter = size // 4
    return [hop(value, "fsdp", size, lambda i: (i + k * quarter) % size) for k in (1, 2, 3)]


def sum_shards_beside(value, size, first_work, second_work):
    step = 1
    while step < size // 8:
        value = value + hop(value, "fsdp", size, lambda i: i ^ step)
        step *= 2
    recv = hop(value, "fsdp", size, lambda i: i ^ step)
    done = first_work(value)
    recv, done = lax.optimization_barrier((recv, done))
    value = value + recv
    recv = quarters(value, size)
    more = second_work(value)
    recv, more = lax.optimization_barrier((recv, more))
    return sum_quarter(value, recv), done, more


def exchange(value):
    return lax.all_to_all(value, "group", split_axis=0, concat_axis=0, tiled=True)


def local(mol_qkv, pair_list, head_proj, head_out, labels):
    groups = lax.axis_size("group")
    shards = lax.axis_size("fsdp")
    device = lax.axis_index("group")
    mols = mol_qkv.shape[0]
    total_pairs = pair_list.shape[0]
    pairs = total_pairs // groups
    mol = jnp.transpose(mol_qkv, (0, 2, 1, 3))

    blocks = pair_list.T.reshape(3, groups, pairs)
    code = jnp.max(jnp.where(blocks[1] == device, blocks[2], -1), axis=1)
    mine = lax.dynamic_index_in_dim(blocks, device, 1, keepdims=False)
    first, slot = mine[0], mine[1]
    place = jnp.arange(pairs, dtype=jnp.int32)
    same = slot[:, None] == slot[None, :]
    lead = jnp.logical_not(jnp.any(same & (place[None, :] < place[:, None]), axis=1)).astype(jnp.int32)
    mate = jnp.max(jnp.where(same & (place[None, :] > place[:, None]), place[None, :], -1), axis=1)
    targets = labels.astype(F32)
    target_wide = jnp.broadcast_to(targets[:, None], (pairs, 128))

    inc = exchange(pick(pair_list.T, mol, groups))
    inc, lead, mate, target_wide = lax.optimization_barrier((inc, lead, mate, target_wide))
    part, weights, dhidden = forward(first, slot, mol, inc, head_proj, head_out)

    def grads(direction):
        def work(after):
            index, _ = lax.optimization_barrier((first, after))
            return backward(direction, index, slot, mol, inc, head_proj, weights, dhidden)

        return work

    logits_wide, (dq_b, dkv_a), (dq_a, dkv_b) = sum_shards_beside(part, shards, grads(1), grads(0))

    loss_wide = jax.nn.softplus(logits_wide) - target_wide * logits_wide
    out, own = scaled_terms(
        first, slot, lead, mate, logits_wide, target_wide, loss_wide, (dq_b, dkv_b), (dq_a, dkv_a), groups, mols
    )
    back = exchange(out)
    logits = logits_wide[:, 0]
    grads, mean_loss = finish(code, own, back, 1.0 / total_pairs)
    mean_loss = mean_loss.reshape(())
    mol_grad = jnp.transpose(grads, (0, 2, 1, 3))
    return (mol_grad, logits, mean_loss)


def solution(mesh):
    placed = (
        P("group", None, None, "fsdp"),
        P(),
        P("fsdp", None, None),
        P("fsdp", None),
        P("group"),
    )
    return jax.shard_map(
        local,
        mesh=mesh,
        in_specs=placed,
        out_specs=(P("group", None, None, "fsdp"), P("group"), P()),
        check_vma=False,
    )
```

```python
import functools

import jax
import jax.numpy as jnp
from jax import lax
from jax.experimental import pallas as pl
from jax.experimental.pallas import tpu as pltpu
from jax.sharding import PartitionSpec as P

loss_scale = 8192.0
VMEM_BYTES = 24 * 1024 * 1024
LOSS_ROWS = 16
FORWARD_BYTES = int(24 * 1024 * 1024)
FINISH_BYTES = 48 * 1024 * 1024
SECOND_BYTES = 40 * 1024 * 1024
VMEM_ALL = 60 * 1024 * 1024
F32 = jnp.float32
BF16 = jnp.bfloat16
SMEM_SPEC = pl.BlockSpec(memory_space=pltpu.SMEM)
VMEM_SPEC = pl.BlockSpec(memory_space=pltpu.VMEM)
ANY_SPEC = pl.BlockSpec(memory_space=pl.ANY)


def params(limit=VMEM_BYTES):
    return pltpu.CompilerParams(vmem_limit_bytes=limit)


def mm(a, b, ca, cb):
    return lax.dot_general(a, b, (((ca,), (cb,)), ((), ())), preferred_element_type=F32)

HBM_SPEC = pl.BlockSpec(memory_space=pltpu.HBM)


def pick_kernel(pairs_ref, mol_ref, out_ref, hold_ref, in_sems, out_sems):
    slots = out_ref.shape[0]
    mols = mol_ref.shape[0]
    per_owner = pairs_ref.shape[1] // slots
    here = lax.axis_index("group")
    loads = [pltpu.make_async_copy(mol_ref.at[m], hold_ref.at[m], in_sems.at[m]) for m in range(mols)]
    for c in loads:
        c.start()
    members = []
    for s in range(slots):
        member = jnp.int32(0)
        for p in range(s * per_owner, (s + 1) * per_owner):
            member = jnp.where(pairs_ref[1, p] == here, pairs_ref[2, p], member)
        members.append(member)
    for m in range(mols):
        loads[m].wait()
        for s in range(slots):

            @pl.when(members[s] == m)
            def send():
                pltpu.make_async_copy(hold_ref.at[m], out_ref.at[s], out_sems.at[s]).start()

    for s in range(slots):
        pltpu.make_async_copy(hold_ref.at[members[s]], out_ref.at[s], out_sems.at[s]).wait()


def pick(pairs, mol, slots):
    return pl.pallas_call(
        pick_kernel,
        out_shape=jax.ShapeDtypeStruct((slots,) + mol.shape[1:], mol.dtype),
        in_specs=[SMEM_SPEC, HBM_SPEC],
        out_specs=HBM_SPEC,
        scratch_shapes=[
            pltpu.VMEM(mol.shape, mol.dtype),
            pltpu.SemaphoreType.DMA((mol.shape[0],)),
            pltpu.SemaphoreType.DMA((slots,)),
        ],
        compiler_params=params(VMEM_ALL),
        name="pick_rows",
    )(pairs, mol)


def load_units(ids, first_ref, slot_ref, mol_ref, inc_ref, heads, hd, directions):
    units = []
    for h in range(heads):
        cols = slice(h * hd, (h + 1) * hd)
        for j, p in enumerate(ids):
            a, s = first_ref[p], slot_ref[p]
            for d in directions:
                if d == 0:
                    rows = (mol_ref[a, 0, :, cols], inc_ref[s, 1, :, cols], inc_ref[s, 2, :, cols])
                else:
                    rows = (inc_ref[s, 0, :, cols], mol_ref[a, 1, :, cols], mol_ref[a, 2, :, cols])
                units.append((j, d, h) + rows)
    return units


def forward_kernel(
    group, first_ref, slot_ref, home_ref, inc_ref, proj_ref, readout_ref, lp_ref, w_ref, dh_ref, mol_ref, sems
):
    pairs = lp_ref.shape[0]
    mols = home_ref.shape[0]

    def load(m, part, parts):
        at = pl.ds(part, parts)
        return pltpu.make_async_copy(home_ref.at[m, at], mol_ref.at[m, at], sems.at[part, m])

    for part, parts in ((0, 1), (1, 2)):
        for m in range(mols):
            load(m, part, parts).start()
    for m in range(mols):
        load(m, 0, 1).wait()
    length = mol_ref.shape[2]
    heads, hd, _ = proj_ref.shape
    inv_root = hd ** (-0.5)
    readouts = [readout_ref[h : h + 1, :] * (1.0 / length) for h in range(heads)]

    def step(i, carry):
        ids = [i * group + j for j in range(group)]
        units, weights, context = [], [], []
        for direction in (0, 1):
            if direction == 1:

                @pl.when(i == 0)
                def land():
                    for m in range(mols):
                        load(m, 1, 2).wait()

            here = load_units(ids, first_ref, slot_ref, mol_ref, inc_ref, heads, hd, (direction,))
            scores = [mm(u[4], u[3], 1, 1) for u in here]
            fresh = []
            for sc in scores:
                lifted = jnp.exp((sc - jnp.max(sc, axis=0, keepdims=True)) * inv_root)
                fresh.append(lifted * (1.0 / jnp.sum(lifted, axis=0, keepdims=True)))
            context.append([mm(w.astype(BF16), u[5], 0, 0).astype(BF16) for w, u in zip(fresh, here)])
            units.append(here)
            weights.append(fresh)
        totals = [None] * group
        dhidden = []
        for h in range(heads):
            mine = [context[d][h * group + j] for d in (0, 1) for j in range(group)]
            hidden = mm(jnp.concatenate(mine, axis=0), proj_ref[h], 1, 0)
            sig = 0.5 + 0.5 * jnp.tanh(0.5 * hidden)
            act = hidden * sig
            for n in range(2 * group):
                rows = jnp.sum(act[n * length : (n + 1) * length], axis=0, keepdims=True) * readouts[h]
                j = n % group
                totals[j] = rows if totals[j] is None else totals[j] + rows
            dhidden.append(((sig + act * (1.0 - sig)) * readouts[h]).astype(BF16))
        for j, p in enumerate(ids):
            total = jnp.sum(totals[j], axis=1, keepdims=True)
            lp_ref[pl.ds(p, 1), :] = jnp.broadcast_to(total, (1, lp_ref.shape[1]))
        for d in (0, 1):
            for n, (j, _, h, *_) in enumerate(units[d]):
                at = d * group + j
                w_ref[d, ids[j], h] = weights[d][n]
                dh_ref[d, ids[j], h] = dhidden[h][at * length : (at + 1) * length]
        return carry

    lax.fori_loop(0, pairs // group, step, 0)


def forward(first, slot, mol, inc, proj, readout):
    pairs = first.shape[0]
    length = mol.shape[2]
    heads, _, width = proj.shape
    return pl.pallas_call(
        functools.partial(forward_kernel, min(16, pairs)),
        out_shape=(
            jax.ShapeDtypeStruct((pairs, 128), F32),
            jax.ShapeDtypeStruct((2, pairs, heads, length, length), F32),
            jax.ShapeDtypeStruct((2, pairs, heads, length, width), BF16),
            jax.ShapeDtypeStruct(mol.shape, mol.dtype),
        ),
        in_specs=[SMEM_SPEC] * 2 + [HBM_SPEC] + [VMEM_SPEC] * 3,
        out_specs=(VMEM_SPEC,) * 4,
        scratch_shapes=[pltpu.SemaphoreType.DMA((2, mol.shape[0]))],
        compiler_params=params(FORWARD_BYTES),
        name="pair_forward",
    )(first, slot, mol, inc, proj, readout)


def backward_kernel(direction, group, first_ref, slot_ref, mol_ref, inc_ref, proj_ref, w_ref, dh_ref, dq_ref, dkv_ref):
    pairs, length, _ = dq_ref.shape
    heads, hd, _ = proj_ref.shape
    inv_root = hd ** (-0.5)

    def step(i, carry):
        ids = [i * group + j for j in range(group)]
        units = load_units(ids, first_ref, slot_ref, mol_ref, inc_ref, heads, hd, (direction,))
        weights = [w_ref[0, ids[u[0]], u[2]] for u in units]
        dcontext = []
        for h in range(heads):
            dhidden = jnp.concatenate([dh_ref[0, p, h] for p in ids], axis=0)
            whole = mm(dhidden, proj_ref[h], 1, 1).astype(BF16)
            dcontext += [whole[j * length : (j + 1) * length] for j in range(group)]
        dvalues = [mm(w.astype(BF16), dc, 1, 0).astype(BF16) for w, dc in zip(weights, dcontext)]
        dweights = [mm(u[5], dc, 1, 1) for u, dc in zip(units, dcontext)]
        dscores = []
        for w, dw in zip(weights, dweights):
            inner = jnp.sum(dw * w, axis=0, keepdims=True)
            dscores.append((w * (dw - inner) * inv_root).astype(BF16))
        dqueries = [mm(ds, u[4], 0, 0).astype(BF16) for ds, u in zip(dscores, units)]
        dkeys = [mm(ds, u[3], 1, 0).astype(BF16) for ds, u in zip(dscores, units)]
        for n, (j, _, h, *_) in enumerate(units):
            cols = slice(h * hd, (h + 1) * hd)
            dq_ref[ids[j], :, cols] = dqueries[n]
            dkv_ref[ids[j], 0, :, cols] = dkeys[n]
            dkv_ref[ids[j], 1, :, cols] = dvalues[n]
        return carry

    lax.fori_loop(0, pairs // group, step, 0)


def backward(direction, first, slot, mol, inc, proj, weights, dhidden):
    pairs = first.shape[0]
    _, parts, length, width = mol.shape
    here = lambda i: (direction, 0, 0, 0, 0)
    return pl.pallas_call(
        functools.partial(backward_kernel, direction, min(16, pairs)),
        grid=(1,),
        out_shape=(
            jax.ShapeDtypeStruct((pairs, length, width), BF16),
            jax.ShapeDtypeStruct((pairs, parts - 1, length, width), BF16),
        ),
        in_specs=[SMEM_SPEC] * 2
        + [VMEM_SPEC] * 3
        + [pl.BlockSpec((1,) + weights.shape[1:], here), pl.BlockSpec((1,) + dhidden.shape[1:], here)],
        out_specs=(VMEM_SPEC,) * 2,
        compiler_params=params(),
        name="pair_backward",
    )(first, slot, mol, inc, proj, weights, dhidden)


def grad_scale(logits, target):
    scale = (0.5 + 0.5 * jnp.tanh(0.5 * logits) - target) * loss_scale
    return jnp.concatenate([scale, scale], axis=1)


def three_parts(value):
    high = value.astype(BF16).astype(F32)
    middle = (value - high).astype(BF16).astype(F32)
    low = value - high - middle
    row = lax.broadcasted_iota(jnp.int32, (LOSS_ROWS, value.shape[1]), 0)
    rows = jnp.where(row == 0, high, jnp.where(row == 1, middle, jnp.where(row == 2, low, 0.0)))
    return rows.astype(BF16)


def scale_kernel(
    first_ref,
    slot_ref,
    lead_ref,
    mate_ref,
    logits_ref,
    target_ref,
    loss_ref,
    dq_ref,
    dkv_ref,
    own_dq_ref,
    own_dkv_ref,
    out_ref,
    own_ref,
    scale_ref,
    hold_ref,
    tail_ref,
    sems,
    tail_sems,
):
    pairs, length, width = dq_ref.shape
    slots, _, hd = out_ref.shape
    heads = width // hd
    rows = 3 * heads * length
    tail_ref[...] = three_parts(jnp.sum(loss_ref[...], axis=0, keepdims=True))
    tails = [
        pltpu.make_async_copy(tail_ref, out_ref.at[s, pl.ds(rows, LOSS_ROWS)], tail_sems.at[s]) for s in range(slots)
    ]
    for c in tails:
        c.start()
    scale_ref[...] = grad_scale(logits_ref[...], target_ref[...])

    def send(p):
        return pltpu.make_async_copy(hold_ref.at[p], out_ref.at[slot_ref[p], pl.ds(0, rows)], sems.at[p])

    def part(p, c):
        return (dq_ref[p] if c == 0 else dkv_ref[p, c - 1]).astype(F32)

    def hold(p, c, value):
        value = value.astype(BF16)
        for h in range(heads):
            at = (c * heads + h) * length
            hold_ref[p, at : at + length] = value[:, h * hd : (h + 1) * hd]

    def step(p, carry):
        mate = mate_ref[p]
        own = scale_ref[pl.ds(p, 1), :]

        @pl.when((lead_ref[p] == 1) & (mate < 0))
        def single():
            for c in range(3):
                hold(p, c, own * part(p, c))
            send(p).start()

        @pl.when((lead_ref[p] == 1) & (mate >= 0))
        def double():
            at = jnp.maximum(mate, 0)
            other = scale_ref[pl.ds(at, 1), :]
            for c in range(3):
                hold(p, c, own * part(p, c) + other * part(at, c))
            send(p).start()

        return carry

    lax.fori_loop(0, pairs, step, 0)
    own_ref[...] = jnp.zeros_like(own_ref)

    def own_step(p, carry):
        a = first_ref[p]
        scale = scale_ref[pl.ds(p, 1), :]
        for c in range(3):
            own_ref[a, c] += scale * (own_dq_ref[p] if c == 0 else own_dkv_ref[p, c - 1]).astype(F32)
        return carry

    lax.fori_loop(0, pairs, own_step, 0)

    def land(p, carry):
        @pl.when(lead_ref[p] == 1)
        def wait():
            send(p).wait()

        return carry

    lax.fori_loop(0, pairs, land, 0)
    for c in tails:
        c.wait()


def scaled_terms(first, slot, lead, mate, logits, target, loss, second, own, slots, mols):
    pairs, length, width = second[0].shape
    hd = logits.shape[1]
    rows = 3 * length * (width // hd)
    return pl.pallas_call(
        scale_kernel,
        out_shape=(
            jax.ShapeDtypeStruct((slots, rows + LOSS_ROWS, hd), BF16),
            jax.ShapeDtypeStruct((mols, 3, length, width), F32),
        ),
        in_specs=[SMEM_SPEC] * 4 + [VMEM_SPEC] * 7,
        out_specs=(HBM_SPEC, VMEM_SPEC),
        scratch_shapes=[
            pltpu.VMEM((pairs, width), F32),
            pltpu.VMEM((pairs, rows, hd), BF16),
            pltpu.VMEM((LOSS_ROWS, hd), BF16),
            pltpu.SemaphoreType.DMA((pairs,)),
            pltpu.SemaphoreType.DMA((slots,)),
        ],
        compiler_params=params(SECOND_BYTES),
        name="scaled_terms",
    )(first, slot, lead, mate, logits, target, loss, *second, *own)


def finish_kernel(scale, code_ref, own_ref, back_ref, out_ref, loss_ref, held_ref, tail_ref, sum_ref, done_ref, sems, tail_sem, out_sems):
    slots, _, hd = back_ref.shape
    mols, parts, length, width = own_ref.shape
    heads = width // hd
    block = heads * length
    codes = [code_ref[s] for s in range(slots)]

    def load(c, s):
        rows = pl.ds(c * block, block)
        return pltpu.make_async_copy(back_ref.at[s, rows], held_ref.at[s, rows], sems.at[c, s])

    for c in range(parts):
        for s in range(slots):
            pl.when(codes[s] >= 0)(load(c, s).start)
    tail = pltpu.make_async_copy(back_ref.at[:, pl.ds(parts * block, LOSS_ROWS)], tail_ref, tail_sem)
    tail.start()

    for c in range(parts):
        sum_ref[...] = own_ref[:, c]
        for s in range(slots):

            @pl.when(codes[s] >= 0)
            def add():
                load(c, s).wait()
                for h in range(heads):
                    at = c * block + h * length
                    cols = slice(h * hd, (h + 1) * hd)
                    sum_ref[jnp.maximum(codes[s], 0), :, cols] += held_ref[s, at : at + length].astype(F32)

        done_ref[c] = sum_ref[...].astype(BF16)
        pltpu.make_async_copy(done_ref.at[c], out_ref.at[:, c], out_sems.at[c]).start()

    tail.wait()
    total = tail_ref[0].astype(F32)
    for s in range(1, slots):
        total = total + tail_ref[s].astype(F32)
    loss_ref[0, 0] = jnp.sum(total[:, :1]) * scale
    for c in range(parts):
        pltpu.make_async_copy(done_ref.at[c], out_ref.at[:, c], out_sems.at[c]).wait()


def finish(code, own, back, scale):
    mols, parts, length, width = own.shape
    slots, rows, hd = back.shape
    return pl.pallas_call(
        functools.partial(finish_kernel, scale),
        out_shape=(jax.ShapeDtypeStruct(own.shape, BF16), jax.ShapeDtypeStruct((1, 1), F32)),
        in_specs=[SMEM_SPEC, VMEM_SPEC, HBM_SPEC],
        out_specs=(HBM_SPEC, SMEM_SPEC),
        scratch_shapes=[
            pltpu.VMEM((slots, rows - LOSS_ROWS, hd), BF16),
            pltpu.VMEM((slots, LOSS_ROWS, hd), BF16),
            pltpu.VMEM((mols, length, width), F32),
            pltpu.VMEM((parts, mols, length, width), BF16),
            pltpu.SemaphoreType.DMA((parts, slots)),
            pltpu.SemaphoreType.DMA,
            pltpu.SemaphoreType.DMA((parts,)),
        ],
        compiler_params=params(FINISH_BYTES),
        name="finish_parts",
    )(code, own, back)


def hop(value, axis, size, change):
    return lax.ppermute(value, axis, [(i, change(i)) for i in range(size)])


def sum_quarter(value, recv):
    near, far, last = recv
    return (value + far) + (near + last)


def quarters(value, size):
    quarter = size // 4
    return [hop(value, "fsdp", size, lambda i: (i + k * quarter) % size) for k in (1, 2, 3)]


def sum_shards_beside(value, size, first_work, second_work):
    step = 1
    while step < size // 8:
        value = value + hop(value, "fsdp", size, lambda i: i ^ step)
        step *= 2
    recv = hop(value, "fsdp", size, lambda i: i ^ step)
    done = first_work(value)
    recv, done = lax.optimization_barrier((recv, done))
    value = value + recv
    recv = quarters(value, size)
    more = second_work(value)
    recv, more = lax.optimization_barrier((recv, more))
    return sum_quarter(value, recv), done, more


def exchange(value):
    return lax.all_to_all(value, "group", split_axis=0, concat_axis=0, tiled=True)


def local(mol_qkv, pair_list, head_proj, head_out, labels):
    groups = lax.axis_size("group")
    shards = lax.axis_size("fsdp")
    device = lax.axis_index("group")
    mols = mol_qkv.shape[0]
    total_pairs = pair_list.shape[0]
    pairs = total_pairs // groups
    mol = jnp.transpose(mol_qkv, (0, 2, 1, 3))

    blocks = pair_list.T.reshape(3, groups, pairs)
    code = jnp.max(jnp.where(blocks[1] == device, blocks[2], -1), axis=1)
    mine = lax.dynamic_index_in_dim(blocks, device, 1, keepdims=False)
    first, slot = mine[0], mine[1]
    place = jnp.arange(pairs, dtype=jnp.int32)
    same = slot[:, None] == slot[None, :]
    lead = jnp.logical_not(jnp.any(same & (place[None, :] < place[:, None]), axis=1)).astype(jnp.int32)
    mate = jnp.max(jnp.where(same & (place[None, :] > place[:, None]), place[None, :], -1), axis=1)
    targets = labels.astype(F32)
    target_wide = jnp.broadcast_to(targets[:, None], (pairs, 128))

    inc = exchange(pick(pair_list.T, mol, groups))
    inc, lead, mate, target_wide = lax.optimization_barrier((inc, lead, mate, target_wide))
    part, weights, dhidden, near = forward(first, slot, pltpu.with_memory_space_constraint(mol, pltpu.HBM), inc, head_proj, head_out)

    def grads(direction):
        def work(after):
            index, _ = lax.optimization_barrier((first, after))
            return backward(direction, index, slot, near, inc, head_proj, weights, dhidden)

        return work

    logits_wide, (dq_b, dkv_a), (dq_a, dkv_b) = sum_shards_beside(part, shards, grads(1), grads(0))

    loss_wide = jax.nn.softplus(logits_wide) - target_wide * logits_wide
    out, own = scaled_terms(
        first, slot, lead, mate, logits_wide, target_wide, loss_wide, (dq_b, dkv_b), (dq_a, dkv_a), groups, mols
    )
    back = exchange(out)
    logits = logits_wide[:, 0]
    grads, mean_loss = finish(code, own, back, 1.0 / total_pairs)
    mean_loss = mean_loss.reshape(())
    mol_grad = jnp.transpose(grads, (0, 2, 1, 3))
    return (mol_grad, logits, mean_loss)


def solution(mesh):
    placed = (
        P("group", None, None, "fsdp"),
        P(),
        P("fsdp", None, None),
        P("fsdp", None),
        P("group"),
    )
    return jax.shard_map(
        local,
        mesh=mesh,
        in_specs=placed,
        out_specs=(P("group", None, None, "fsdp"), P("group"), P()),
        check_vma=False,
    )
```

```python
import functools

import jax
import jax.numpy as jnp
from jax import lax
from jax.experimental import pallas as pl
from jax.experimental.pallas import tpu as pltpu
from jax.sharding import PartitionSpec as P

loss_scale = 8192.0
VMEM_BYTES = 24 * 1024 * 1024
LOSS_ROWS = 16
FINISH_BYTES = 48 * 1024 * 1024
SECOND_BYTES = 40 * 1024 * 1024
VMEM_ALL = 60 * 1024 * 1024
F32 = jnp.float32
BF16 = jnp.bfloat16
SMEM_SPEC = pl.BlockSpec(memory_space=pltpu.SMEM)
VMEM_SPEC = pl.BlockSpec(memory_space=pltpu.VMEM)
ANY_SPEC = pl.BlockSpec(memory_space=pl.ANY)


def params(limit=VMEM_BYTES):
    return pltpu.CompilerParams(vmem_limit_bytes=limit)


def mm(a, b, ca, cb):
    return lax.dot_general(a, b, (((ca,), (cb,)), ((), ())), preferred_element_type=F32)

HBM_SPEC = pl.BlockSpec(memory_space=pltpu.HBM)


def pick_kernel(pairs_ref, mol_ref, out_ref, hold_ref, in_sems, out_sems):
    slots = out_ref.shape[0]
    mols = mol_ref.shape[0]
    per_owner = pairs_ref.shape[1] // slots
    here = lax.axis_index("group")
    loads = [pltpu.make_async_copy(mol_ref.at[m], hold_ref.at[m], in_sems.at[m]) for m in range(mols)]
    for c in loads:
        c.start()
    members = []
    for s in range(slots):
        member = jnp.int32(0)
        for p in range(s * per_owner, (s + 1) * per_owner):
            member = jnp.where(pairs_ref[1, p] == here, pairs_ref[2, p], member)
        members.append(member)
    for m in range(mols):
        loads[m].wait()
        for s in range(slots):

            @pl.when(members[s] == m)
            def send():
                pltpu.make_async_copy(hold_ref.at[m], out_ref.at[s], out_sems.at[s]).start()

    for s in range(slots):
        pltpu.make_async_copy(hold_ref.at[members[s]], out_ref.at[s], out_sems.at[s]).wait()


def pick(pairs, mol, slots):
    return pl.pallas_call(
        pick_kernel,
        out_shape=jax.ShapeDtypeStruct((slots,) + mol.shape[1:], mol.dtype),
        in_specs=[SMEM_SPEC, HBM_SPEC],
        out_specs=HBM_SPEC,
        scratch_shapes=[
            pltpu.VMEM(mol.shape, mol.dtype),
            pltpu.SemaphoreType.DMA((mol.shape[0],)),
            pltpu.SemaphoreType.DMA((slots,)),
        ],
        compiler_params=params(VMEM_ALL),
        name="pick_rows",
    )(pairs, mol)


def load_units(ids, first_ref, slot_ref, mol_ref, inc_ref, heads, hd, directions):
    units = []
    for h in range(heads):
        cols = slice(h * hd, (h + 1) * hd)
        for j, p in enumerate(ids):
            a, s = first_ref[p], slot_ref[p]
            for d in directions:
                if d == 0:
                    rows = (mol_ref[a, 0, :, cols], inc_ref[s, 1, :, cols], inc_ref[s, 2, :, cols])
                else:
                    rows = (inc_ref[s, 0, :, cols], mol_ref[a, 1, :, cols], mol_ref[a, 2, :, cols])
                units.append((j, d, h) + rows)
    return units


def forward_kernel(group, first_ref, slot_ref, mol_ref, inc_ref, proj_ref, readout_ref, lp_ref, w_ref, dh_ref):
    pairs = lp_ref.shape[0]
    length = mol_ref.shape[2]
    heads, hd, _ = proj_ref.shape
    inv_root = hd ** (-0.5)
    readouts = [readout_ref[h : h + 1, :] * (1.0 / length) for h in range(heads)]

    def step(i, carry):
        ids = [i * group + j for j in range(group)]
        units = load_units(ids, first_ref, slot_ref, mol_ref, inc_ref, heads, hd, (0, 1))
        scores = [mm(u[4], u[3], 1, 1) for u in units]
        weights = []
        for sc in scores:
            lifted = jnp.exp((sc - jnp.max(sc, axis=0, keepdims=True)) * inv_root)
            weights.append((lifted * (1.0 / jnp.sum(lifted, axis=0, keepdims=True))).astype(BF16))
        context = [mm(w, u[5], 0, 0).astype(BF16) for w, u in zip(weights, units)]
        count = len(units) // heads
        totals = [None] * group
        dhidden = []
        for h in range(heads):
            hidden = mm(jnp.concatenate(context[h * count : (h + 1) * count], axis=0), proj_ref[h], 1, 0)
            sig = 0.5 + 0.5 * jnp.tanh(0.5 * hidden)
            act = hidden * sig
            for j in range(group):
                rows = jnp.sum(act[2 * j * length : (2 * j + 2) * length], axis=0, keepdims=True) * readouts[h]
                totals[j] = rows if totals[j] is None else totals[j] + rows
            dhidden.append(((sig + act * (1.0 - sig)) * readouts[h]).astype(BF16))
        for j, p in enumerate(ids):
            total = jnp.sum(totals[j], axis=1, keepdims=True)
            lp_ref[pl.ds(p, 1), :] = jnp.broadcast_to(total, (1, lp_ref.shape[1]))
        for n, (j, d, h, *_) in enumerate(units):
            at = n - h * count
            w_ref[d, ids[j], h] = weights[n]
            dh_ref[d, ids[j], h] = dhidden[h][at * length : (at + 1) * length]
        return carry

    lax.fori_loop(0, pairs // group, step, 0)


def forward(first, slot, mol, inc, proj, readout):
    pairs = first.shape[0]
    length = mol.shape[2]
    heads, _, width = proj.shape
    return pl.pallas_call(
        functools.partial(forward_kernel, min(16, pairs)),
        out_shape=(
            jax.ShapeDtypeStruct((pairs, 128), F32),
            jax.ShapeDtypeStruct((2, pairs, heads, length, length), BF16),
            jax.ShapeDtypeStruct((2, pairs, heads, length, width), BF16),
        ),
        in_specs=[SMEM_SPEC] * 2 + [VMEM_SPEC] * 4,
        out_specs=(VMEM_SPEC,) * 3,
        compiler_params=params(),
        name="pair_forward",
    )(first, slot, mol, inc, proj, readout)


def backward_kernel(direction, group, first_ref, slot_ref, mol_ref, inc_ref, proj_ref, w_ref, dh_ref, dq_ref, dkv_ref):
    pairs, length, _ = dq_ref.shape
    heads, hd, _ = proj_ref.shape
    inv_root = hd ** (-0.5)

    def step(i, carry):
        ids = [i * group + j for j in range(group)]
        units = load_units(ids, first_ref, slot_ref, mol_ref, inc_ref, heads, hd, (direction,))
        weights = [w_ref[0, ids[u[0]], u[2]] for u in units]
        dcontext = []
        for h in range(heads):
            dhidden = jnp.concatenate([dh_ref[0, p, h] for p in ids], axis=0)
            whole = mm(dhidden, proj_ref[h], 1, 1).astype(BF16)
            dcontext += [whole[j * length : (j + 1) * length] for j in range(group)]
        dvalues = [mm(w, dc, 1, 0).astype(BF16) for w, dc in zip(weights, dcontext)]
        dweights = [mm(u[5], dc, 1, 1) for u, dc in zip(units, dcontext)]
        dscores = []
        for w, dw in zip(weights, dweights):
            w = w.astype(F32)
            inner = jnp.sum(dw * w, axis=0, keepdims=True)
            dscores.append((w * (dw - inner) * inv_root).astype(BF16))
        dqueries = [mm(ds, u[4], 0, 0).astype(BF16) for ds, u in zip(dscores, units)]
        dkeys = [mm(ds, u[3], 1, 0).astype(BF16) for ds, u in zip(dscores, units)]
        for n, (j, _, h, *_) in enumerate(units):
            cols = slice(h * hd, (h + 1) * hd)
            dq_ref[ids[j], :, cols] = dqueries[n]
            dkv_ref[ids[j], 0, :, cols] = dkeys[n]
            dkv_ref[ids[j], 1, :, cols] = dvalues[n]
        return carry

    lax.fori_loop(0, pairs // group, step, 0)


def backward(direction, first, slot, mol, inc, proj, weights, dhidden):
    pairs = first.shape[0]
    _, parts, length, width = mol.shape
    here = lambda i: (direction, 0, 0, 0, 0)
    return pl.pallas_call(
        functools.partial(backward_kernel, direction, min(16, pairs)),
        grid=(1,),
        out_shape=(
            jax.ShapeDtypeStruct((pairs, length, width), BF16),
            jax.ShapeDtypeStruct((pairs, parts - 1, length, width), BF16),
        ),
        in_specs=[SMEM_SPEC] * 2
        + [VMEM_SPEC] * 3
        + [pl.BlockSpec((1,) + weights.shape[1:], here), pl.BlockSpec((1,) + dhidden.shape[1:], here)],
        out_specs=(VMEM_SPEC,) * 2,
        compiler_params=params(),
        name="pair_backward",
    )(first, slot, mol, inc, proj, weights, dhidden)


def grad_scale(logits, target):
    scale = (0.5 + 0.5 * jnp.tanh(0.5 * logits) - target) * loss_scale
    return jnp.concatenate([scale, scale], axis=1)


def three_parts(value):
    high = value.astype(BF16).astype(F32)
    middle = (value - high).astype(BF16).astype(F32)
    low = value - high - middle
    row = lax.broadcasted_iota(jnp.int32, (LOSS_ROWS, value.shape[1]), 0)
    rows = jnp.where(row == 0, high, jnp.where(row == 1, middle, jnp.where(row == 2, low, 0.0)))
    return rows.astype(BF16)


def scale_kernel(
    first_ref,
    slot_ref,
    lead_ref,
    mate_ref,
    logits_ref,
    target_ref,
    loss_ref,
    dq_ref,
    dkv_ref,
    own_dq_ref,
    own_dkv_ref,
    out_ref,
    own_ref,
    scale_ref,
    hold_ref,
    tail_ref,
    sems,
    tail_sems,
):
    pairs, length, width = dq_ref.shape
    slots, _, hd = out_ref.shape
    heads = width // hd
    rows = 3 * heads * length
    tail_ref[...] = three_parts(jnp.sum(loss_ref[...], axis=0, keepdims=True))
    tails = [
        pltpu.make_async_copy(tail_ref, out_ref.at[s, pl.ds(rows, LOSS_ROWS)], tail_sems.at[s]) for s in range(slots)
    ]
    for c in tails:
        c.start()
    scale_ref[...] = grad_scale(logits_ref[...], target_ref[...])

    def send(p):
        return pltpu.make_async_copy(hold_ref.at[p], out_ref.at[slot_ref[p], pl.ds(0, rows)], sems.at[p])

    def part(p, c):
        return (dq_ref[p] if c == 0 else dkv_ref[p, c - 1]).astype(F32)

    def hold(p, c, value):
        value = value.astype(BF16)
        for h in range(heads):
            at = (c * heads + h) * length
            hold_ref[p, at : at + length] = value[:, h * hd : (h + 1) * hd]

    def step(p, carry):
        mate = mate_ref[p]
        own = scale_ref[pl.ds(p, 1), :]

        @pl.when((lead_ref[p] == 1) & (mate < 0))
        def single():
            for c in range(3):
                hold(p, c, own * part(p, c))
            send(p).start()

        @pl.when((lead_ref[p] == 1) & (mate >= 0))
        def double():
            at = jnp.maximum(mate, 0)
            other = scale_ref[pl.ds(at, 1), :]
            for c in range(3):
                hold(p, c, own * part(p, c) + other * part(at, c))
            send(p).start()

        return carry

    lax.fori_loop(0, pairs, step, 0)
    own_ref[...] = jnp.zeros_like(own_ref)

    def own_step(p, carry):
        a = first_ref[p]
        scale = scale_ref[pl.ds(p, 1), :]
        for c in range(3):
            own_ref[a, c] += scale * (own_dq_ref[p] if c == 0 else own_dkv_ref[p, c - 1]).astype(F32)
        return carry

    lax.fori_loop(0, pairs, own_step, 0)

    def land(p, carry):
        @pl.when(lead_ref[p] == 1)
        def wait():
            send(p).wait()

        return carry

    lax.fori_loop(0, pairs, land, 0)
    for c in tails:
        c.wait()


def scaled_terms(first, slot, lead, mate, logits, target, loss, second, own, slots, mols):
    pairs, length, width = second[0].shape
    hd = logits.shape[1]
    rows = 3 * length * (width // hd)
    return pl.pallas_call(
        scale_kernel,
        out_shape=(
            jax.ShapeDtypeStruct((slots, rows + LOSS_ROWS, hd), BF16),
            jax.ShapeDtypeStruct((mols, 3, length, width), F32),
        ),
        in_specs=[SMEM_SPEC] * 4 + [VMEM_SPEC] * 7,
        out_specs=(HBM_SPEC, VMEM_SPEC),
        scratch_shapes=[
            pltpu.VMEM((pairs, width), F32),
            pltpu.VMEM((pairs, rows, hd), BF16),
            pltpu.VMEM((LOSS_ROWS, hd), BF16),
            pltpu.SemaphoreType.DMA((pairs,)),
            pltpu.SemaphoreType.DMA((slots,)),
        ],
        compiler_params=params(SECOND_BYTES),
        name="scaled_terms",
    )(first, slot, lead, mate, logits, target, loss, *second, *own)


def finish_kernel(scale, code_ref, own_ref, back_ref, out_ref, loss_ref, held_ref, tail_ref, sum_ref, done_ref, sems, tail_sem, out_sems):
    slots, _, hd = back_ref.shape
    mols, parts, length, width = own_ref.shape
    heads = width // hd
    block = heads * length
    codes = [code_ref[s] for s in range(slots)]

    def load(c, s):
        rows = pl.ds(c * block, block)
        return pltpu.make_async_copy(back_ref.at[s, rows], held_ref.at[s, rows], sems.at[c, s])

    for c in range(parts):
        for s in range(slots):
            pl.when(codes[s] >= 0)(load(c, s).start)
    tail = pltpu.make_async_copy(back_ref.at[:, pl.ds(parts * block, LOSS_ROWS)], tail_ref, tail_sem)
    tail.start()

    for c in range(parts):
        sum_ref[...] = own_ref[:, c]
        for s in range(slots):

            @pl.when(codes[s] >= 0)
            def add():
                load(c, s).wait()
                for h in range(heads):
                    at = c * block + h * length
                    cols = slice(h * hd, (h + 1) * hd)
                    sum_ref[jnp.maximum(codes[s], 0), :, cols] += held_ref[s, at : at + length].astype(F32)

        done_ref[c] = sum_ref[...].astype(BF16)
        pltpu.make_async_copy(done_ref.at[c], out_ref.at[:, c], out_sems.at[c]).start()

    tail.wait()
    total = tail_ref[0].astype(F32)
    for s in range(1, slots):
        total = total + tail_ref[s].astype(F32)
    loss_ref[0, 0] = jnp.sum(total[:, :1]) * scale
    for c in range(parts):
        pltpu.make_async_copy(done_ref.at[c], out_ref.at[:, c], out_sems.at[c]).wait()


def finish(code, own, back, scale):
    mols, parts, length, width = own.shape
    slots, rows, hd = back.shape
    return pl.pallas_call(
        functools.partial(finish_kernel, scale),
        out_shape=(jax.ShapeDtypeStruct(own.shape, BF16), jax.ShapeDtypeStruct((1, 1), F32)),
        in_specs=[SMEM_SPEC, VMEM_SPEC, HBM_SPEC],
        out_specs=(HBM_SPEC, SMEM_SPEC),
        scratch_shapes=[
            pltpu.VMEM((slots, rows - LOSS_ROWS, hd), BF16),
            pltpu.VMEM((slots, LOSS_ROWS, hd), BF16),
            pltpu.VMEM((mols, length, width), F32),
            pltpu.VMEM((parts, mols, length, width), BF16),
            pltpu.SemaphoreType.DMA((parts, slots)),
            pltpu.SemaphoreType.DMA,
            pltpu.SemaphoreType.DMA((parts,)),
        ],
        compiler_params=params(FINISH_BYTES),
        name="finish_parts",
    )(code, own, back)


def hop(value, axis, size, change):
    return lax.ppermute(value, axis, [(i, change(i)) for i in range(size)])


def sum_quarter(value, recv):
    near, far, last = recv
    return (value + far) + (near + last)


def quarters(value, size):
    quarter = size // 4
    return [hop(value, "fsdp", size, lambda i: (i + k * quarter) % size) for k in (1, 2, 3)]


def sum_shards_beside(value, size, first_work, second_work):
    step = 1
    while step < size // 8:
        value = value + hop(value, "fsdp", size, lambda i: i ^ step)
        step *= 2
    recv = hop(value, "fsdp", size, lambda i: i ^ step)
    done = first_work(value)
    recv, done = lax.optimization_barrier((recv, done))
    value = value + recv
    recv = quarters(value, size)
    more = second_work(value)
    recv, more = lax.optimization_barrier((recv, more))
    return sum_quarter(value, recv), done, more


def exchange(value):
    return lax.all_to_all(value, "group", split_axis=0, concat_axis=0, tiled=True)


def local(mol_qkv, pair_list, head_proj, head_out, labels):
    groups = lax.axis_size("group")
    shards = lax.axis_size("fsdp")
    device = lax.axis_index("group")
    mols = mol_qkv.shape[0]
    total_pairs = pair_list.shape[0]
    pairs = total_pairs // groups
    mol = jnp.transpose(mol_qkv, (0, 2, 1, 3))

    blocks = pair_list.T.reshape(3, groups, pairs)
    code = jnp.max(jnp.where(blocks[1] == device, blocks[2], -1), axis=1)
    mine = lax.dynamic_index_in_dim(blocks, device, 1, keepdims=False)
    first, slot = mine[0], mine[1]
    place = jnp.arange(pairs, dtype=jnp.int32)
    same = slot[:, None] == slot[None, :]
    lead = jnp.logical_not(jnp.any(same & (place[None, :] < place[:, None]), axis=1)).astype(jnp.int32)
    mate = jnp.max(jnp.where(same & (place[None, :] > place[:, None]), place[None, :], -1), axis=1)
    targets = labels.astype(F32)
    target_wide = jnp.broadcast_to(targets[:, None], (pairs, 128))

    inc = exchange(pick(pair_list.T, mol, groups))
    inc, lead, mate, target_wide = lax.optimization_barrier((inc, lead, mate, target_wide))
    part, weights, dhidden = forward(first, slot, mol, inc, head_proj, head_out)

    def grads(direction):
        def work(after):
            index, _ = lax.optimization_barrier((first, after))
            return backward(direction, index, slot, mol, inc, head_proj, weights, dhidden)

        return work

    logits_wide, (dq_b, dkv_a), (dq_a, dkv_b) = sum_shards_beside(part, shards, grads(1), grads(0))

    loss_wide = jax.nn.softplus(logits_wide) - target_wide * logits_wide
    out, own = scaled_terms(
        first, slot, lead, mate, logits_wide, target_wide, loss_wide, (dq_b, dkv_b), (dq_a, dkv_a), groups, mols
    )
    back = exchange(out)
    logits = logits_wide[:, 0]
    grads, mean_loss = finish(code, own, back, 1.0 / total_pairs)
    mean_loss = mean_loss.reshape(())
    mol_grad = jnp.transpose(grads, (0, 2, 1, 3))
    return (mol_grad, logits, mean_loss)


def solution(mesh):
    placed = (
        P("group", None, None, "fsdp"),
        P(),
        P("fsdp", None, None),
        P("fsdp", None),
        P("group"),
    )
    return jax.shard_map(
        local,
        mesh=mesh,
        in_specs=placed,
        out_specs=(P("group", None, None, "fsdp"), P("group"), P()),
        check_vma=False,
    )
```
